128 devices in a mesh: wide: 32 (over y, z, core), narrow: 4 (over x).
Axes of the slice: x: 4, y: 4, z: 4, core: 2. Of those that a mesh axis runs over, the one named last changes fastest.
Arguments:
- matrix: float32 [8, 2097152], P(None, ('wide', 'narrow')), may hold values from -6 to 6
- flips: int32 [2097152], P(('wide', 'narrow')), may hold values 0 or 1
- owners: int32 [131072, 1], P(('wide', 'narrow')), may hold values from 0 to 127; in each aligned block of 1024 rows (0 to 1023, 1024 to 2047, ...) at most 16 rows name the same one
- offsets: int32 [131072], P(('wide', 'narrow')), may hold values from 0 to 16383, as said below
Outputs:
- sketch: float32 [8, 131072], P(None, ('wide', 'narrow'))
- partial_gram: float32 [64, 128], P(None, ('wide', 'narrow'))
The draws below stay inside these ranges and needn't reach their ends.
Inputs may be any that keep to these rules, and one draw needn't show every extreme that they name: `owners`: within the 1024 sampled rows of one device, no owner value appears more than 16 times, and some value appears exactly 16 times. Within the 1024 sampled rows of one device, each value of offsets // 128 appears exactly 1024 // 128 times.
All inputs are finite; a program needn't handle non-finite values. No bound on the sum of `flips` on one device may be relied on, other than what follows from the above.
Results may differ from the reference program's by a relative error of at most 0.00011.
Values sent between devices are 32-bit elements; how exact they have to be, the bound alone decides.
No kernel may reach another device: no remote copies, remote signals or barrier semaphores. Data moves between devices by JAX's collectives and lax.ppermute only.
A program may use at most 64 MiB of HBM per device.

```python
import math
import jax
import jax.numpy as jnp
import numpy as np
from jax import lax

LOCAL = 16384
COLS = 8
PICK_DEV = 1024
ROWS = 2097152
PICKS = 131072
CAP = 16
N_WIDE = 32
N_NARROW = 4


def draw_offsets(key, part):
    device_count = N_WIDE * N_NARROW
    section = LOCAL // device_count
    first_key = jax.random.fold_in(key, 11)
    second_key = jax.random.fold_in(key, 23)
    base = (jnp.arange(PICK_DEV, dtype=jnp.int32) % device_count).astype(jnp.int32)
    block_keys = jax.random.split(first_key, device_count)
    buckets = jax.vmap(lambda one_key: jax.random.permutation(one_key, base))(block_keys).reshape(-1)
    within = jax.random.randint(second_key, (PICK_DEV * device_count,), 0, section, dtype=jnp.int32)
    return (buckets * section + within).astype(jnp.int32)


def place_ends(entries, own_key, low, high):
    longest = entries.shape.index(max(entries.shape))
    spots = []
    for shift in (0, 1):
        where = [jax.random.randint(jax.random.fold_in(own_key, axis), (), 0, length) for axis, length in enumerate(entries.shape)]
        where[longest] = (where[longest] + shift) % entries.shape[longest]
        spots.append(tuple(where))
    return entries.at[spots[0]].set(low).at[spots[1]].set(high)


def block_scale(stream_key, dims, cuts, smallest, largest):
    def one(position, blocks):
        steps = jax.random.uniform(jax.random.fold_in(jax.random.fold_in(stream_key, 6), position), (blocks,), jnp.float32, smallest / len(cuts), largest / len(cuts))
        return jnp.repeat(jnp.exp(steps), dims[position] // blocks).reshape((-1,) + (1,) * (len(dims) - position - 1))

    factor_of = one(*cuts[0])
    for cut in cuts[1:]:
        factor_of = factor_of * one(*cut)
    return factor_of


def assign_block(rng, own, number, rows, count, top, bound, slope):
    order = jax.random.permutation(rng, count)
    crowded, ordinary = load_shares(count, rows * top, bound, slope, True), load_shares(count, rows * top, bound, slope, False)
    places = jnp.arange(count)

    def named(sizes, turn):
        used = int((sizes > 0).sum())
        fixed = max(1, used // 4)
        moved = fixed + (places - fixed + turn * (used - fixed)) % max(1, count - fixed)
        return jnp.zeros((count,), jnp.int32).at[order[jnp.where(places < fixed, places, moved)]].set(jnp.asarray(sizes, jnp.int32))

    sizes = jnp.where(number % 4 == 0, named(crowded, number // 4), named(ordinary, number - number // 4 - 1))
    mixed = jax.random.permutation(jax.random.fold_in(own, 3), count)
    donor, taker = mixed[0:count // 2 * 2:2], mixed[1:count // 2 * 2:2]
    margin = jnp.minimum(sizes[donor] - 1, bound - sizes[taker]) // 2
    margin = jnp.where((donor == order[0]) | (taker == order[0]) | (sizes[taker] == 0), 0, jnp.maximum(margin, 0))
    moved = jax.random.randint(jax.random.fold_in(own, 4), (count // 2,), 0, 1 << 20) % (margin + 1)
    sizes = sizes.at[donor].add(-moved).at[taker].add(moved)
    items = jnp.searchsorted(jnp.cumsum(sizes), jnp.arange(rows * top), side="right").astype(jnp.int32)
    listing = items.reshape(top, rows).T
    listing = listing[jax.random.permutation(jax.random.fold_in(own, 1), rows)]
    turn = jax.random.randint(jax.random.fold_in(own, 2), (rows, 1), 0, top)
    return jnp.take_along_axis(listing, (jnp.arange(top)[None, :] + turn) % top, axis=1)


def load_shares(number_of, total, most, skew, full):
    portions = [(1 << 20) // math.isqrt(standing ** skew) + 1 for standing in range(1, number_of + 1)]
    largest = most if full else min(most, max(-(-total // number_of), total * portions[0] // sum(portions)))
    least = 1 if total - largest >= number_of - 1 else 0
    given, spare = [largest] + [least] * (number_of - 1), total - largest - least * (number_of - 1)
    while spare > 0:
        free = [i for i in range(1, number_of) if given[i] < largest] or [i for i in range(1, number_of) if given[i] < most]
        pool, left = sum([portions[i] for i in free]), spare
        for i in free:
            more = min(most - given[i], max(1, left * portions[i] // pool), spare)
            given[i] = given[i] + more
            spare = spare - more
    return np.array(given)


def gaussian(stream_key, shape, spread, most, cuts=(), kind=jnp.bfloat16):
    loudness = block_scale(stream_key, shape, cuts, -0.22, 0.18) if cuts else 1.0
    result = jax.random.normal(stream_key, shape, jnp.float32) * spread * loudness
    return jnp.minimum(jnp.maximum(result, -most), most).astype(kind)


def setup_inputs(seed: int = 0) -> dict:
    streams_of = jax.random.split(jax.random.key(seed), 5)
    matrix = gaussian(streams_of[0], (COLS, ROWS), 1.0, 6.0, ((1, 128),), jnp.float32)
    flips = place_ends((jax.random.randint(streams_of[1], (ROWS,), 0, 2) < 1).astype(jnp.int32), jax.random.fold_in(streams_of[1], 1), 0, 1)
    owners_keys = jax.random.split(jax.random.fold_in(streams_of[2], 1), PICKS // PICK_DEV)
    owners_turns = jax.random.permutation(jax.random.fold_in(streams_of[2], 3), PICKS // PICK_DEV)
    owners = jax.vmap(lambda own, number: assign_block(jax.random.fold_in(streams_of[2], 2), own, number, PICK_DEV, N_WIDE * N_NARROW, 1, CAP, 2))(owners_keys, owners_turns).reshape((PICKS, 1))
    offsets = draw_offsets(jax.random.fold_in(streams_of[4], 71), 0)
    return {"matrix": matrix, "flips": flips, "owners": owners, "offsets": offsets}


def sylvester(count):
    left_index = lax.broadcasted_iota(jnp.int32, (count, count), 0)
    right_index = lax.broadcasted_iota(jnp.int32, (count, count), 1)
    common = jnp.bitwise_and(left_index, right_index)
    parity = jnp.zeros((count, count), jnp.int32)
    for level in range(count.bit_length() - 1):
        parity = parity + jnp.right_shift(common, level) % 2
    return (1 - 2 * (parity % 2)).astype(jnp.float32) / math.sqrt(count)

def local_transform(block):
    columns, length = block.shape
    remaining = length.bit_length() - 1
    stride = 1
    while remaining > 0:
        digit_bits = min(7, remaining)
        remaining = remaining - digit_bits
        count = 2 ** digit_bits
        table = sylvester(count)
        if stride == 1:
            block = jnp.dot(block.reshape(-1, count), table, precision=lax.Precision.HIGHEST)
        else:
            shaped = block.reshape(-1, count, stride)
            block = jnp.einsum('pnq,nm->pmq', shaped, table, precision=lax.Precision.HIGHEST)
        block = block.reshape(columns, length)
        stride = stride * count
    return block

def reference(matrix, flips, owners, offsets):
    signed = matrix * (2 * flips - 1).astype(jnp.float32)[None, :]
    mixed = local_transform(signed)
    rows = (owners[:, 0] * LOCAL + offsets).astype(jnp.int32)
    sketch = mixed[:, rows]
    blocks = sketch.reshape(COLS, N_WIDE * N_NARROW, PICK_DEV)
    gram = jnp.einsum('adk,bdk->abd', blocks, blocks, precision=lax.Precision.HIGHEST) / PICK_DEV
    return (sketch, gram.reshape(COLS * COLS, N_WIDE * N_NARROW))
```

```python
import functools
import math

import jax
import jax.numpy as jnp
from jax import lax
from jax.experimental import pallas as pl
from jax.experimental.pallas import tpu as pltpu
from jax.sharding import PartitionSpec as P

LANES = 128
SLOTS = 8
COLS = 8
CHUNK = COLS + 1
PICKS = LANES * SLOTS
VMEM = pl.BlockSpec(memory_space=pltpu.VMEM)
ACROSS = ("wide", "narrow")


def walsh(tiles):
    span = 1
    while span < len(tiles):
        out = list(tiles)
        for i in range(len(tiles)):
            if not i & span:
                out[i] = tiles[i] + tiles[i | span]
                out[i | span] = tiles[i] - tiles[i | span]
        tiles = out
        span *= 2
    return tiles


def one_hot(section):
    rows = lax.broadcasted_iota(jnp.int32, (LANES, section.shape[1]), 0)
    return rows == section


def split(values):
    high = values.astype(jnp.bfloat16)
    return high, (values - high.astype(jnp.float32)).astype(jnp.bfloat16)


def send_kernel(matrix, flips, owners, offsets, message, rank_out, signs, mid):
    place = offsets[...]
    section = lax.shift_right_logical(place, 7)
    hot = one_hot(section).astype(jnp.float32)
    before = lax.broadcasted_iota(jnp.int32, (LANES, LANES), 0) < lax.broadcasted_iota(jnp.int32, (LANES, LANES), 1)
    table = jnp.concatenate([before.astype(jnp.float32), jnp.ones((LANES, LANES), jnp.float32)], axis=1)
    table = table.astype(jnp.bfloat16)
    carry = jnp.zeros((LANES, LANES), jnp.float32)
    ranks = []
    for t in range(SLOTS):
        part = hot[:, t * LANES : (t + 1) * LANES]
        sums = jnp.dot(part.astype(jnp.bfloat16), table, preferred_element_type=jnp.float32)
        ranks.append(jnp.sum(part * (sums[:, :LANES] + carry), axis=0, keepdims=True))
        carry = carry + sums[:, LANES:]
    rank = jnp.concatenate(ranks, axis=1)
    rank_out[...] = rank.astype(jnp.int32)
    slot = lax.broadcasted_iota(jnp.int32, (SLOTS, PICKS), 0) == rank.astype(jnp.int32)
    low = (place & (LANES - 1)).astype(jnp.float32)
    wanted = jnp.concatenate(
        [jnp.where(slot, owners[...].astype(jnp.float32), 0.0), jnp.where(slot, low, 0.0)], axis=0
    )
    found = lax.dot_general(
        hot.astype(jnp.bfloat16),
        wanted.astype(jnp.bfloat16),
        (((1,), (1,)), ((), ())),
        preferred_element_type=jnp.float32,
    )
    rows = lax.broadcasted_iota(jnp.int32, (LANES, SLOTS), 0).astype(jnp.float32) * float(LANES)
    rows = found[:, :SLOTS] * float(LANES * LANES) + rows + found[:, SLOTS:]
    rows = jnp.concatenate([rows, jnp.zeros((LANES, LANES - SLOTS), jnp.float32)], axis=1)
    message[pl.ds(COLS, LANES, stride=CHUNK), :] = rows

    scale = 1.0 / math.sqrt(float(LANES) ** 3)
    signs[...] = jnp.where(flips[...] == 1, scale, -scale)
    for j in range(8):
        tiles = []
        for i in range(16):
            f = i * 8 + j
            tiles.append(matrix[:, f * LANES : (f + 1) * LANES] * signs[f : f + 1, :])
        for i, tile in enumerate(walsh(tiles)):
            mid[i * 8 + j] = tile
    for i in range(16):
        for j, tile in enumerate(walsh([mid[i * 8 + j] for j in range(8)])):
            message[pl.ds((i * 8 + j) * CHUNK, COLS), :] = tile


def sign_table(index):
    bit = lambda b: 1.0 - 2.0 * (lax.shift_right_logical(index, b) & 1).astype(jnp.float32)
    row = lax.broadcasted_iota(jnp.int32, (8, index.shape[1]), 0)
    block = jnp.ones((8, index.shape[1]), jnp.float32)
    for b in range(3):
        block = block * jnp.where(lax.shift_right_logical(row, b) & 1 == 1, bit(b), 1.0)
    blocks = [block]
    for b in range(3, 7):
        factor = bit(b)
        blocks = blocks + [block * factor for block in blocks]
    return jnp.concatenate(blocks, axis=0)


def answer_kernel(message, reply, left, right, signs):
    wanted = message[pl.ds(COLS, LANES, stride=CHUNK), :]
    wanted = wanted.T[:SLOTS, :].astype(jnp.int32)
    for r in range(SLOTS):
        index = wanted[r : r + 1, :]
        cut = slice(r * LANES, (r + 1) * LANES)
        table = sign_table(index & (LANES - 1)).astype(jnp.bfloat16)
        right[:LANES, cut] = table
        right[LANES:, cut] = table
        signs[:, cut] = sign_table(lax.shift_right_logical(index, 14))
    for pair in range(LANES // 2):
        tile = jnp.concatenate(
            [message[pl.ds(d * CHUNK, COLS), :] for d in (2 * pair, 2 * pair + 1)], axis=0
        )
        high, low = split(tile)
        left[pl.ds(pair * 16, 16), :LANES] = high
        left[pl.ds(pair * 16, 16), LANES:] = low
    answers = []
    width = 256
    for n in range(PICKS // width):
        cut = slice(n * width, (n + 1) * width)
        total = jnp.zeros((COLS, width), jnp.float32)
        for m in range(4):
            part = jnp.dot(left[m * 256 : (m + 1) * 256, :], right[:, cut], preferred_element_type=jnp.float32)
            for d in range(32):
                total = total + part[d * COLS : (d + 1) * COLS, :] * signs[m * 32 + d : m * 32 + d + 1, cut]
        answers += [total[:, :LANES], total[:, LANES:]]
    answers.append(jnp.zeros((LANES - SLOTS * COLS, LANES), jnp.float32))
    reply[...] = jnp.concatenate(answers, axis=0).T


def finish_kernel(reply, offsets, rank, sketch, gram):
    section = lax.shift_right_logical(offsets[...], 7)
    hot = one_hot(section).astype(jnp.float32).astype(jnp.bfloat16)
    high, low = split(reply[...].T[: SLOTS * COLS, :])
    parts = jnp.dot(high, hot, preferred_element_type=jnp.float32) + jnp.dot(
        low, hot, preferred_element_type=jnp.float32
    )
    place = rank[...]
    total = jnp.zeros((COLS, PICKS), jnp.float32)
    for r in range(SLOTS):
        total = total + jnp.where(place == r, parts[r * COLS : (r + 1) * COLS, :], 0.0)
    sketch[...] = total
    products = []
    for a in range(COLS):
        product = total * total[a : a + 1, :]
        products.append(sum(product[:, t * LANES : (t + 1) * LANES] for t in range(SLOTS)))
    products = jnp.concatenate(products + [jnp.zeros((LANES - COLS * COLS, LANES), jnp.float32)], axis=0)
    gram[...] = jnp.sum(products.T, axis=0, keepdims=True) * (1.0 / PICKS)


def on_device(matrix, flips, owners, offsets):
    f32 = jnp.float32
    offsets = offsets.reshape(1, PICKS)
    message, rank = pl.pallas_call(
        send_kernel,
        name="transform_sections",
        out_shape=(
            jax.ShapeDtypeStruct((LANES * CHUNK, LANES), f32),
            jax.ShapeDtypeStruct((1, PICKS), jnp.int32),
        ),
        in_specs=[VMEM] * 4,
        out_specs=(VMEM, VMEM),
        scratch_shapes=[pltpu.VMEM((LANES, LANES), f32), pltpu.VMEM((LANES, COLS, LANES), f32)],
        compiler_params=pltpu.CompilerParams(vmem_limit_bytes=32 * 2**20),
    )(matrix, flips.reshape(LANES, LANES), owners.reshape(1, PICKS), offsets)
    message = lax.all_to_all(
        message.reshape(LANES, 1, CHUNK * LANES), ACROSS, split_axis=0, concat_axis=0, tiled=True
    ).reshape(LANES * CHUNK, LANES)
    reply = pl.pallas_call(
        answer_kernel,
        name="answer",
        out_shape=jax.ShapeDtypeStruct((LANES, LANES), f32),
        in_specs=[VMEM],
        out_specs=VMEM,
        scratch_shapes=[
            pltpu.VMEM((LANES * COLS, 2 * LANES), jnp.bfloat16),
            pltpu.VMEM((2 * LANES, PICKS), jnp.bfloat16),
            pltpu.VMEM((LANES, PICKS), f32),
        ],
        compiler_params=pltpu.CompilerParams(vmem_limit_bytes=32 * 2**20),
    )(message)
    reply = lax.all_to_all(
        reply.reshape(LANES, 1, LANES), ACROSS, split_axis=0, concat_axis=0, tiled=True
    ).reshape(LANES, LANES)
    sketch, gram = pl.pallas_call(
        finish_kernel,
        name="finish",
        out_shape=(jax.ShapeDtypeStruct((COLS, PICKS), f32), jax.ShapeDtypeStruct((1, LANES), f32)),
        in_specs=[VMEM] * 3,
        out_specs=(VMEM, VMEM),
        compiler_params=pltpu.CompilerParams(vmem_limit_bytes=32 * 2**20),
    )(reply, offsets, rank)
    return sketch, gram[:, : COLS * COLS].reshape(COLS * COLS, 1)


def solution(mesh):
    in_specs = (P(None, ACROSS), P(ACROSS), P(ACROSS, None), P(ACROSS))
    out_specs = (P(None, ACROSS), P(None, ACROSS))
    return jax.shard_map(on_device, mesh=mesh, in_specs=in_specs, out_specs=out_specs, check_vma=False)
```

```python
import math

import jax
import jax.numpy as jnp
from jax import lax
from jax.experimental import pallas as pl
from jax.experimental.pallas import tpu as pltpu
from jax.sharding import PartitionSpec as P

LANES = 128
SLOTS = 8
COLS = 8
CHUNK = COLS + 1
PICKS = LANES * SLOTS
PIECES = 4
VMEM = pl.BlockSpec(memory_space=pltpu.VMEM)
HBM = pl.BlockSpec(memory_space=pltpu.HBM)
ACROSS = ("wide", "narrow")


def walsh(tiles):
    span = 1
    while span < len(tiles):
        out = list(tiles)
        for i in range(len(tiles)):
            if not i & span:
                out[i] = tiles[i] + tiles[i | span]
                out[i | span] = tiles[i] - tiles[i | span]
        tiles = out
        span *= 2
    return tiles


def one_hot(section):
    rows = lax.broadcasted_iota(jnp.int32, (LANES, section.shape[1]), 0)
    return rows == section


def split(values):
    high = values.astype(jnp.bfloat16)
    return high, (values - high.astype(jnp.float32)).astype(jnp.bfloat16)


def send_kernel(
    matrix_hbm, flips_hbm, owners_hbm, offsets_hbm, message, slots_out, matrix, flips, owners, offsets, mid, arrived
):
    copies = [
        pltpu.make_async_copy(source, target, arrived.at[i])
        for i, (source, target) in enumerate(
            ((offsets_hbm, offsets), (owners_hbm, owners), (flips_hbm, flips))
        )
    ]
    width = matrix.shape[1] // PIECES
    for p in range(PIECES):
        cut = pl.ds(p * width, width)
        copies.append(pltpu.make_async_copy(matrix_hbm.at[:, cut], matrix.at[:, cut], arrived.at[3 + p]))
    for copy in copies:
        copy.start()

    copies[0].wait()
    place = offsets[...]
    section = lax.shift_right_logical(place, 7)
    hot = one_hot(section).astype(jnp.float32)
    before = lax.broadcasted_iota(jnp.int32, (LANES, LANES), 0) < lax.broadcasted_iota(jnp.int32, (LANES, LANES), 1)
    table = jnp.concatenate([before.astype(jnp.float32), jnp.ones((LANES, LANES), jnp.float32)], axis=1)
    table = table.astype(jnp.bfloat16)
    carry = jnp.zeros((LANES, LANES), jnp.float32)
    ranks = []
    for t in range(SLOTS):
        part = hot[:, t * LANES : (t + 1) * LANES]
        sums = jnp.dot(part.astype(jnp.bfloat16), table, preferred_element_type=jnp.float32)
        ranks.append(jnp.sum(part * (sums[:, :LANES] + carry), axis=0, keepdims=True))
        carry = carry + sums[:, LANES:]
    rank = jnp.concatenate(ranks, axis=1).astype(jnp.int32)
    slots_out[...] = section * SLOTS + rank
    slot = lax.broadcasted_iota(jnp.int32, (SLOTS, PICKS), 0) == rank
    low = (place & (LANES - 1)).astype(jnp.float32)
    copies[1].wait()
    wanted = jnp.concatenate(
        [jnp.where(slot, owners[...].astype(jnp.float32), 0.0), jnp.where(slot, low, 0.0)], axis=0
    )
    found = lax.dot_general(
        hot.astype(jnp.bfloat16),
        wanted.astype(jnp.bfloat16),
        (((1,), (1,)), ((), ())),
        preferred_element_type=jnp.float32,
    )
    rows = lax.broadcasted_iota(jnp.int32, (LANES, SLOTS), 0).astype(jnp.float32) * float(LANES)
    rows = found[:, :SLOTS] * float(LANES * LANES) + rows + found[:, SLOTS:]
    rows = jnp.concatenate([rows, jnp.zeros((LANES, LANES - SLOTS), jnp.float32)], axis=1)
    message[pl.ds(COLS, LANES, stride=CHUNK), :] = rows

    scale = 1.0 / math.sqrt(float(LANES) ** 3)
    copies[2].wait()
    signs = jnp.where(flips[...] == 1, scale, -scale)
    for i in range(16):
        if i * PIECES % 16 == 0:
            copies[3 + i * PIECES // 16].wait()
        tiles = []
        for f in range(i * 8, i * 8 + 8):
            tiles.append(matrix[:, f * LANES : (f + 1) * LANES] * signs[f : f + 1, :])
        for j, tile in enumerate(walsh(tiles)):
            mid[i * 8 + j] = tile
    for j in range(8):
        for i, tile in enumerate(walsh([mid[i * 8 + j] for i in range(16)])):
            message[pl.ds((i * 8 + j) * CHUNK, COLS), :] = tile


def sign_table(index):
    bit = lambda b: 1.0 - 2.0 * (lax.shift_right_logical(index, b) & 1).astype(jnp.float32)
    row = lax.broadcasted_iota(jnp.int32, (8, index.shape[1]), 0)
    block = jnp.ones((8, index.shape[1]), jnp.float32)
    for b in range(3):
        block = block * jnp.where(lax.shift_right_logical(row, b) & 1 == 1, bit(b), 1.0)
    blocks = [block]
    for b in range(3, 7):
        factor = bit(b)
        blocks = blocks + [block * factor for block in blocks]
    return jnp.concatenate(blocks, axis=0)


def answer_kernel(message, reply, left, right, signs):
    wanted = message[pl.ds(COLS, LANES, stride=CHUNK), :]
    wanted = wanted.T[:SLOTS, :].astype(jnp.int32)
    for r in range(SLOTS):
        index = wanted[r : r + 1, :]
        cut = slice(r * LANES, (r + 1) * LANES)
        table = sign_table(index & (LANES - 1)).astype(jnp.bfloat16)
        right[:LANES, cut] = table
        right[LANES:, cut] = table
        signs[:, cut] = sign_table(lax.shift_right_logical(index, 14))
    for pair in range(LANES // 2):
        tile = jnp.concatenate(
            [message[pl.ds(d * CHUNK, COLS), :] for d in (2 * pair, 2 * pair + 1)], axis=0
        )
        high, low = split(tile)
        left[pl.ds(pair * 16, 16), :LANES] = high
        left[pl.ds(pair * 16, 16), LANES:] = low
    answers = []
    width = 256
    for n in range(PICKS // width):
        cut = slice(n * width, (n + 1) * width)
        total = jnp.zeros((COLS, width), jnp.float32)
        for m in range(4):
            part = jnp.dot(left[m * 256 : (m + 1) * 256, :], right[:, cut], preferred_element_type=jnp.float32)
            for d in range(32):
                total = total + part[d * COLS : (d + 1) * COLS, :] * signs[m * 32 + d : m * 32 + d + 1, cut]
        answers += [total[:, :LANES], total[:, LANES:]]
    answers.append(jnp.zeros((LANES - SLOTS * COLS, LANES), jnp.float32))
    reply[...] = jnp.concatenate(answers, axis=0).T


def finish_kernel(reply, slots, sketch_hbm, gram_hbm, sketch, gram, sent):
    place = slots[...]
    hot = one_hot(lax.shift_right_logical(place, 3)).astype(jnp.float32).astype(jnp.bfloat16)
    high, low = split(reply[...].T[: SLOTS * COLS, :])
    parts = jnp.dot(high, hot, preferred_element_type=jnp.float32) + jnp.dot(
        low, hot, preferred_element_type=jnp.float32
    )
    place = place & (SLOTS - 1)
    total = jnp.zeros((COLS, PICKS), jnp.float32)
    for r in range(SLOTS):
        total = total + jnp.where(place == r, parts[r * COLS : (r + 1) * COLS, :], 0.0)
    sketch[...] = total
    first = pltpu.make_async_copy(sketch, sketch_hbm, sent.at[0])
    first.start()
    products = []
    for a in range(COLS):
        product = total * total[a : a + 1, :]
        products.append(sum(product[:, t * LANES : (t + 1) * LANES] for t in range(SLOTS)))
    products = jnp.concatenate(products + [jnp.zeros((LANES - COLS * COLS, LANES), jnp.float32)], axis=0)
    products = jnp.sum(products.T, axis=0, keepdims=True) * (1.0 / PICKS)
    gram[...] = products[:, : COLS * COLS]
    second = pltpu.make_async_copy(gram, gram_hbm, sent.at[1])
    second.start()
    first.wait()
    second.wait()


def on_device(matrix, flips, owners, offsets):
    f32, i32 = jnp.float32, jnp.int32
    params = pltpu.CompilerParams(vmem_limit_bytes=32 * 2**20)
    message, slots = pl.pallas_call(
        send_kernel,
        name="transform_sections",
        out_shape=(
            jax.ShapeDtypeStruct((LANES * CHUNK, LANES), f32),
            jax.ShapeDtypeStruct((1, PICKS), i32),
        ),
        in_specs=[HBM] * 4,
        out_specs=(VMEM, VMEM),
        scratch_shapes=[
            pltpu.VMEM((COLS, LANES * LANES), f32),
            pltpu.VMEM((LANES, LANES), i32),
            pltpu.VMEM((1, PICKS), i32),
            pltpu.VMEM((1, PICKS), i32),
            pltpu.VMEM((LANES, COLS, LANES), f32),
            pltpu.SemaphoreType.DMA((3 + PIECES,)),
        ],
        compiler_params=params,
    )(
        *(
            pltpu.with_memory_space_constraint(operand, pltpu.HBM)
            for operand in (
                matrix,
                flips.reshape(LANES, LANES),
                owners.reshape(1, PICKS),
                offsets.reshape(1, PICKS),
            )
        )
    )
    message = lax.all_to_all(
        message.reshape(LANES, 1, CHUNK * LANES), ACROSS, split_axis=0, concat_axis=0, tiled=True
    ).reshape(LANES * CHUNK, LANES)
    reply = pl.pallas_call(
        answer_kernel,
        name="answer",
        out_shape=jax.ShapeDtypeStruct((LANES, LANES), f32),
        in_specs=[VMEM],
        out_specs=VMEM,
        scratch_shapes=[
            pltpu.VMEM((LANES * COLS, 2 * LANES), jnp.bfloat16),
            pltpu.VMEM((2 * LANES, PICKS), jnp.bfloat16),
            pltpu.VMEM((LANES, PICKS), f32),
        ],
        compiler_params=params,
    )(message)
    reply = lax.all_to_all(
        reply.reshape(LANES, 1, LANES), ACROSS, split_axis=0, concat_axis=0, tiled=True
    ).reshape(LANES, LANES)
    sketch, gram = pl.pallas_call(
        finish_kernel,
        name="finish",
        out_shape=(jax.ShapeDtypeStruct((COLS, PICKS), f32), jax.ShapeDtypeStruct((1, COLS * COLS), f32)),
        in_specs=[VMEM] * 2,
        out_specs=(HBM, HBM),
        scratch_shapes=[
            pltpu.VMEM((COLS, PICKS), f32),
            pltpu.VMEM((1, COLS * COLS), f32),
            pltpu.SemaphoreType.DMA((2,)),
        ],
        compiler_params=params,
    )(reply, slots)
    return sketch, gram.reshape(COLS * COLS, 1)


def solution(mesh):
    in_specs = (P(None, ACROSS), P(ACROSS), P(ACROSS, None), P(ACROSS))
    out_specs = (P(None, ACROSS), P(None, ACROSS))
    return jax.shard_map(on_device, mesh=mesh, in_specs=in_specs, out_specs=out_specs, check_vma=False)
```

```python
import math

import jax
import jax.numpy as jnp
from jax import lax
from jax.experimental import pallas as pl
from jax.experimental.pallas import tpu as pltpu
from jax.sharding import Mesh
from jax.sharding import PartitionSpec as P

LANES = 128
CHIPS = 64
HALVES = 2
SLOTS = 8
COLS = 8
CHUNK = HALVES * COLS + 1
PICKS = LANES * SLOTS
PIECES = 4
FIRST = 42
VMEM = pl.BlockSpec(memory_space=pltpu.VMEM)
HBM = pl.BlockSpec(memory_space=pltpu.HBM)


def device(chip, core):
    return (chip >> 2) * 8 + core * 4 + (chip & 3)


def exchange(rows):
    groups = [[device(j ^ FIRST, core) for j in range(CHIPS)] for core in range(2)]
    parts = rows.reshape(CHIPS, 1, -1)
    parts = lax.all_to_all(parts, "all", split_axis=0, concat_axis=0, tiled=True, axis_index_groups=groups)
    return parts.reshape(rows.shape)


def other_core(value):
    return lax.ppermute(value, "all", [(i, i ^ 4) for i in range(2 * CHIPS)])


def walsh(tiles):
    span = 1
    while span < len(tiles):
        out = list(tiles)
        for i in range(len(tiles)):
            if not i & span:
                out[i] = tiles[i] + tiles[i | span]
                out[i | span] = tiles[i] - tiles[i | span]
        tiles = out
        span *= 2
    return tiles


def one_hot(index, count):
    rows = lax.broadcasted_iota(jnp.int32, (count, index.shape[1]), 0)
    return (rows == index).astype(jnp.float32)


def split(values):
    high = values.astype(jnp.bfloat16)
    return high, (values - high.astype(jnp.float32)).astype(jnp.bfloat16)


def requests(place, owner):
    section = lax.shift_right_logical(place, 7)
    part = lax.shift_right_logical(section, 1) ^ FIRST
    hot = one_hot((section & 1) * CHIPS + part, LANES)
    before = lax.broadcasted_iota(jnp.int32, (LANES, LANES), 0) < lax.broadcasted_iota(jnp.int32, (LANES, LANES), 1)
    table = jnp.concatenate([before.astype(jnp.float32), jnp.ones((LANES, LANES), jnp.float32)], axis=1)
    table = table.astype(jnp.bfloat16)
    carry = jnp.zeros((LANES, LANES), jnp.float32)
    ranks = []
    for t in range(SLOTS):
        some = hot[:, t * LANES : (t + 1) * LANES]
        sums = jnp.dot(some.astype(jnp.bfloat16), table, preferred_element_type=jnp.float32)
        ranks.append(jnp.sum(some * (sums[:, :LANES] + carry), axis=0, keepdims=True))
        carry = carry + sums[:, LANES:]
    rank = jnp.concatenate(ranks, axis=1).astype(jnp.int32)
    slot = lax.broadcasted_iota(jnp.int32, (SLOTS, PICKS), 0) == rank
    low = (place & (LANES - 1)).astype(jnp.float32)
    wanted = jnp.concatenate(
        [jnp.where(slot, owner.astype(jnp.float32), 0.0), jnp.where(slot, low, 0.0)], axis=0
    )
    found = lax.dot_general(
        hot.astype(jnp.bfloat16),
        wanted.astype(jnp.bfloat16),
        (((1,), (1,)), ((), ())),
        preferred_element_type=jnp.float32,
    )
    row = lax.broadcasted_iota(jnp.int32, (LANES, SLOTS), 0)
    section_of = (((row & (CHIPS - 1)) ^ FIRST) * 2 + lax.shift_right_logical(row, 6)).astype(jnp.float32)
    rows = found[:, :SLOTS] * float(LANES * LANES) + section_of * float(LANES) + found[:, SLOTS:]
    return rank, jnp.concatenate([rows[:CHIPS], rows[CHIPS:]], axis=1)


def send_kernel(
    matrix_hbm, flips_hbm, owners_hbm, offsets_hbm, message, own, slots, matrix, flips, owners, offsets, mid, arrived
):
    copies = [
        pltpu.make_async_copy(source, target, arrived.at[i])
        for i, (source, target) in enumerate(
            ((offsets_hbm, offsets), (owners_hbm, owners), (flips_hbm, flips))
        )
    ]
    width = matrix.shape[1] // PIECES
    for p in range(PIECES):
        cut = pl.ds(p * width, width)
        copies.append(pltpu.make_async_copy(matrix_hbm.at[:, cut], matrix.at[:, cut], arrived.at[3 + p]))
    for copy in copies:
        copy.start()

    copies[0].wait()
    copies[1].wait()
    place = offsets[...]
    rank, rows = requests(place, owners[...])
    own[...] = jnp.concatenate([rows, jnp.zeros((CHIPS, LANES - HALVES * SLOTS), jnp.float32)], axis=1)
    section = lax.shift_right_logical(place, 7)
    part = lax.shift_right_logical(section, 1) ^ FIRST
    slots[...] = part * (HALVES * SLOTS) + (section & 1) * SLOTS + rank

    scale = 1.0 / math.sqrt(float(LANES) ** 3)
    copies[2].wait()
    signs = jnp.where(flips[...] == 1, scale, -scale)
    for i in range(16):
        if i * PIECES % 16 == 0:
            copies[3 + i * PIECES // 16].wait()
        tiles = []
        for f in range(i * 8, i * 8 + 8):
            tiles.append(matrix[:, f * LANES : (f + 1) * LANES] * signs[f : f + 1, :])
        for j, tile in enumerate(walsh(tiles)):
            mid[i * 8 + j] = tile
    for j in range(8):
        for i, tile in enumerate(walsh([mid[i * 8 + j] for i in range(16)])):
            section = i * 8 + j
            row = ((section >> 1) ^ FIRST) * CHUNK + (section & 1) * COLS
            message[pl.ds(row, COLS), :] = tile


def ask_kernel(_, own, owners, offsets, message):
    _, rows = requests(offsets[...], owners[...])
    count = HALVES * SLOTS
    rows = jnp.concatenate(
        [jnp.zeros((CHIPS, count), jnp.float32), rows, jnp.zeros((CHIPS, LANES - 2 * count), jnp.float32)], axis=1
    )
    message[pl.ds(CHUNK - 1, CHIPS, stride=CHUNK), :] = own[...] + rows


def bit_sign(index, bit):
    return 1.0 - 2.0 * (lax.shift_right_logical(index, bit) & 1).astype(jnp.float32)


def sign_table(index, bits):
    row = lax.broadcasted_iota(jnp.int32, (8, index.shape[1]), 0)
    block = jnp.ones((8, index.shape[1]), jnp.float32)
    for b in range(3):
        block = block * jnp.where(lax.shift_right_logical(row, b) & 1 == 1, bit_sign(index, b), 1.0)
    blocks = [block]
    for b in range(3, bits):
        factor = bit_sign(index, b)
        blocks = blocks + [block * factor for block in blocks]
    return jnp.concatenate(blocks, axis=0)


def answer_kernel(message, reply, left, right, signs):
    core = lax.shift_right_logical(lax.axis_index("all"), 2) & 1
    wanted = message[pl.ds(CHUNK - 1, CHIPS, stride=CHUNK), :]
    wanted = jnp.concatenate([wanted, pltpu.roll(wanted, LANES - HALVES * SLOTS, 1)], axis=0)
    wanted = wanted.T[: HALVES * SLOTS, :].astype(jnp.int32)
    factors = []
    for n in range(HALVES * SLOTS):
        index = wanted[n : n + 1, :]
        cut = slice(n * LANES, (n + 1) * LANES)
        table = sign_table(index & (LANES - 1), 7).astype(jnp.bfloat16)
        right[:LANES, cut] = table
        right[LANES:, cut] = table
        owner = lax.shift_right_logical(index, 14)
        chip = lax.shift_right_logical(owner, 3) * 4 + (owner & 3)
        signs[:, cut] = sign_table(chip, 6)
        factor = bit_sign(owner & (core * 4), 2)
        for b in range(6):
            if FIRST >> b & 1:
                factor = factor * bit_sign(chip, b)
        factors.append(factor)
    for half in range(HALVES):
        for pair in range(CHIPS // 2):
            tile = jnp.concatenate(
                [message[pl.ds(j * CHUNK + half * COLS, COLS), :] for j in (2 * pair, 2 * pair + 1)], axis=0
            )
            high, low = split(tile)
            left[half, pl.ds(pair * 16, 16), :LANES] = high
            left[half, pl.ds(pair * 16, 16), LANES:] = low
    answers = []
    width = 256
    for half in range(HALVES):
        for n in range(PICKS // width):
            cut = slice(half * PICKS + n * width, half * PICKS + (n + 1) * width)
            total = jnp.zeros((COLS, width), jnp.float32)
            for m in range(2):
                part = jnp.dot(
                    left[half, m * 256 : (m + 1) * 256, :], right[:, cut], preferred_element_type=jnp.float32
                )
                for j in range(32):
                    total = total + part[j * COLS : (j + 1) * COLS, :] * signs[m * 32 + j : m * 32 + j + 1, cut]
            answers += [total[:, :LANES], total[:, LANES:]]
    answers = [answer * factor for answer, factor in zip(answers, factors)]
    answers = jnp.concatenate(answers, axis=0).T
    for t in range(2):
        reply[pl.ds(t, CHIPS, stride=2), :] = answers[t * CHIPS : (t + 1) * CHIPS, :]


def finish_kernel(reply, other, slots, sketch_hbm, gram_hbm, sketch, gram, sent):
    count = HALVES * SLOTS
    place = slots[...]
    hot = one_hot(lax.shift_right_logical(place, 4), CHIPS).astype(jnp.bfloat16)
    answers = jnp.concatenate(
        [reply[pl.ds(0, CHIPS, stride=2), :], other[pl.ds(1, CHIPS, stride=2), :]], axis=0
    )
    parts = jnp.dot(
        jnp.concatenate(split(answers.T), axis=1),
        jnp.concatenate([hot] * 4, axis=0),
        preferred_element_type=jnp.float32,
    )
    place = place & (count - 1)
    total = jnp.zeros((COLS, PICKS), jnp.float32)
    for n in range(count):
        total = total + jnp.where(place == n, parts[n * COLS : (n + 1) * COLS, :], 0.0)
    sketch[...] = total
    first = pltpu.make_async_copy(sketch, sketch_hbm, sent.at[0])
    first.start()
    products = []
    for a in range(COLS):
        product = total * total[a : a + 1, :]
        products.append(sum(product[:, t * LANES : (t + 1) * LANES] for t in range(SLOTS)))
    products = jnp.concatenate(products + [jnp.zeros((LANES - COLS * COLS, LANES), jnp.float32)], axis=0)
    products = jnp.sum(products.T, axis=0, keepdims=True) * (1.0 / PICKS)
    gram[...] = products[:, : COLS * COLS]
    second = pltpu.make_async_copy(gram, gram_hbm, sent.at[1])
    second.start()
    first.wait()
    second.wait()


def on_device(matrix, flips, owners, offsets):
    f32, i32 = jnp.float32, jnp.int32
    params = pltpu.CompilerParams(vmem_limit_bytes=32 * 2**20)
    owners = owners.reshape(1, PICKS)
    offsets = offsets.reshape(1, PICKS)
    owners_other = other_core(owners)
    offsets_other = other_core(offsets)
    message_shape = jax.ShapeDtypeStruct((CHIPS * CHUNK, LANES), f32)
    message, own, slots = pl.pallas_call(
        send_kernel,
        name="transform_sections",
        out_shape=(
            message_shape,
            jax.ShapeDtypeStruct((CHIPS, LANES), f32),
            jax.ShapeDtypeStruct((1, PICKS), i32),
        ),
        in_specs=[HBM] * 4,
        out_specs=(VMEM, VMEM, VMEM),
        scratch_shapes=[
            pltpu.VMEM((COLS, LANES * LANES), f32),
            pltpu.VMEM((LANES, LANES), i32),
            pltpu.VMEM((1, PICKS), i32),
            pltpu.VMEM((1, PICKS), i32),
            pltpu.VMEM((LANES, COLS, LANES), f32),
            pltpu.SemaphoreType.DMA((3 + PIECES,)),
        ],
        compiler_params=params,
        cost_estimate=pl.CostEstimate(flops=2**22, bytes_accessed=4 * 2**20, transcendentals=0),
    )(
        *(
            pltpu.with_memory_space_constraint(operand, pltpu.HBM)
            for operand in (matrix, flips.reshape(LANES, LANES), owners, offsets)
        )
    )
    message = pl.pallas_call(
        ask_kernel,
        name="other_requests",
        out_shape=message_shape,
        in_specs=[VMEM] * 4,
        out_specs=VMEM,
        input_output_aliases={0: 0},
        compiler_params=params,
    )(message, own, owners_other, offsets_other)
    message = exchange(message)
    reply = pl.pallas_call(
        answer_kernel,
        name="answer",
        out_shape=jax.ShapeDtypeStruct((LANES, LANES), f32),
        in_specs=[VMEM],
        out_specs=VMEM,
        scratch_shapes=[
            pltpu.VMEM((HALVES, CHIPS * COLS, 2 * LANES), jnp.bfloat16),
            pltpu.VMEM((2 * LANES, HALVES * PICKS), jnp.bfloat16),
            pltpu.VMEM((CHIPS, HALVES * PICKS), f32),
        ],
        compiler_params=params,
    )(message)
    reply = exchange(reply)
    sketch, gram = pl.pallas_call(
        finish_kernel,
        name="finish",
        out_shape=(jax.ShapeDtypeStruct((COLS, PICKS), f32), jax.ShapeDtypeStruct((1, COLS * COLS), f32)),
        in_specs=[VMEM] * 3,
        out_specs=(HBM, HBM),
        scratch_shapes=[
            pltpu.VMEM((COLS, PICKS), f32),
            pltpu.VMEM((1, COLS * COLS), f32),
            pltpu.SemaphoreType.DMA((2,)),
        ],
        compiler_params=params,
    )(reply, other_core(reply), slots)
    return sketch, gram.reshape(COLS * COLS, 1)


def solution(mesh):
    flat = Mesh(mesh.devices.reshape(-1), ("all",))
    in_specs = (P(None, "all"), P("all"), P("all", None), P("all"))
    out_specs = (P(None, "all"), P(None, "all"))
    return jax.shard_map(on_device, mesh=flat, in_specs=in_specs, out_specs=out_specs, check_vma=False)
```

```python
import math

import jax
import jax.numpy as jnp
from jax import lax
from jax.experimental import pallas as pl
from jax.experimental.pallas import tpu as pltpu
from jax.sharding import Mesh
from jax.sharding import PartitionSpec as P

LANES = 128
CHIPS = 64
HALVES = 2
SLOTS = 8
COLS = 8
CHUNK = HALVES * COLS + 1
PICKS = LANES * SLOTS
PIECES = 4
FIRST = 42
VMEM = pl.BlockSpec(memory_space=pltpu.VMEM)
HBM = pl.BlockSpec(memory_space=pltpu.HBM)


def device(chip, core):
    return (chip >> 2) * 8 + core * 4 + (chip & 3)


def exchange(rows):
    groups = [[device(j ^ FIRST, core) for j in range(CHIPS)] for core in range(2)]
    parts = rows.reshape(CHIPS, 1, -1)
    parts = lax.all_to_all(parts, "all", split_axis=0, concat_axis=0, tiled=True, axis_index_groups=groups)
    return parts.reshape(rows.shape)


def other_core(value):
    return lax.ppermute(value, "all", [(i, i ^ 4) for i in range(2 * CHIPS)])


def walsh(tiles):
    span = 1
    while span < len(tiles):
        out = list(tiles)
        for i in range(len(tiles)):
            if not i & span:
                out[i] = tiles[i] + tiles[i | span]
                out[i | span] = tiles[i] - tiles[i | span]
        tiles = out
        span *= 2
    return tiles


def one_hot(index, count):
    rows = lax.broadcasted_iota(jnp.int32, (count, index.shape[1]), 0)
    return (rows == index).astype(jnp.float32)


def split(values):
    high = values.astype(jnp.bfloat16)
    return high, (values - high.astype(jnp.float32)).astype(jnp.bfloat16)


def requests(place, owner):
    section = lax.shift_right_logical(place, 7)
    part = lax.shift_right_logical(section, 1) ^ FIRST
    hot = one_hot((section & 1) * CHIPS + part, LANES)
    before = lax.broadcasted_iota(jnp.int32, (LANES, LANES), 0) < lax.broadcasted_iota(jnp.int32, (LANES, LANES), 1)
    table = jnp.concatenate([before.astype(jnp.float32), jnp.ones((LANES, LANES), jnp.float32)], axis=1)
    table = table.astype(jnp.bfloat16)
    carry = jnp.zeros((LANES, LANES), jnp.float32)
    ranks = []
    for t in range(SLOTS):
        some = hot[:, t * LANES : (t + 1) * LANES]
        sums = jnp.dot(some.astype(jnp.bfloat16), table, preferred_element_type=jnp.float32)
        ranks.append(jnp.sum(some * (sums[:, :LANES] + carry), axis=0, keepdims=True))
        carry = carry + sums[:, LANES:]
    rank = jnp.concatenate(ranks, axis=1).astype(jnp.int32)
    slot = lax.broadcasted_iota(jnp.int32, (SLOTS, PICKS), 0) == rank
    low = (place & (LANES - 1)).astype(jnp.float32)
    wanted = jnp.concatenate(
        [jnp.where(slot, owner.astype(jnp.float32), 0.0), jnp.where(slot, low, 0.0)], axis=0
    )
    found = lax.dot_general(
        hot.astype(jnp.bfloat16),
        wanted.astype(jnp.bfloat16),
        (((1,), (1,)), ((), ())),
        preferred_element_type=jnp.float32,
    )
    row = lax.broadcasted_iota(jnp.int32, (LANES, SLOTS), 0)
    section_of = (((row & (CHIPS - 1)) ^ FIRST) * 2 + lax.shift_right_logical(row, 6)).astype(jnp.float32)
    rows = found[:, :SLOTS] * float(LANES * LANES) + section_of * float(LANES) + found[:, SLOTS:]
    return rank, jnp.concatenate([rows[:CHIPS], rows[CHIPS:]], axis=1)


def send_kernel(
    matrix_hbm, flips_hbm, owners_hbm, offsets_hbm, message, own, slots, matrix, flips, owners, offsets, mid, arrived
):
    copies = [
        pltpu.make_async_copy(source, target, arrived.at[i])
        for i, (source, target) in enumerate(
            ((offsets_hbm, offsets), (owners_hbm, owners), (flips_hbm, flips))
        )
    ]
    width = matrix.shape[1] // PIECES
    for p in range(PIECES):
        cut = pl.ds(p * width, width)
        copies.append(pltpu.make_async_copy(matrix_hbm.at[:, cut], matrix.at[:, cut], arrived.at[3 + p]))
    for copy in copies:
        copy.start()

    copies[0].wait()
    copies[1].wait()
    place = offsets[...]
    rank, rows = requests(place, owners[...])
    own[...] = jnp.concatenate([rows, jnp.zeros((CHIPS, LANES - HALVES * SLOTS), jnp.float32)], axis=1)
    section = lax.shift_right_logical(place, 7)
    part = lax.shift_right_logical(section, 1) ^ FIRST
    slots[...] = part * (HALVES * SLOTS) + (section & 1) * SLOTS + rank

    scale = 1.0 / math.sqrt(float(LANES) ** 3)
    copies[2].wait()
    signs = jnp.where(flips[...] == 1, scale, -scale)
    for i in range(16):
        if i * PIECES % 16 == 0:
            copies[3 + i * PIECES // 16].wait()
        tiles = []
        for f in range(i * 8, i * 8 + 8):
            tiles.append(matrix[:, f * LANES : (f + 1) * LANES] * signs[f : f + 1, :])
        for j, tile in enumerate(walsh(tiles)):
            mid[i * 8 + j] = tile
    for j in range(8):
        for i, tile in enumerate(walsh([mid[i * 8 + j] for i in range(16)])):
            section = i * 8 + j
            row = ((section >> 1) ^ FIRST) * CHUNK + (section & 1) * COLS
            message[pl.ds(row, COLS), :] = tile


def ask_kernel(_, own, owners, offsets, message):
    _, rows = requests(offsets[...], owners[...])
    count = HALVES * SLOTS
    rows = jnp.concatenate(
        [jnp.zeros((CHIPS, count), jnp.float32), rows, jnp.zeros((CHIPS, LANES - 2 * count), jnp.float32)], axis=1
    )
    message[pl.ds(CHUNK - 1, CHIPS, stride=CHUNK), :] = own[...] + rows


def bit_sign(index, bit):
    return 1.0 - 2.0 * (lax.shift_right_logical(index, bit) & 1).astype(jnp.float32)


def sign_table(index, bits):
    row = lax.broadcasted_iota(jnp.int32, (8, index.shape[1]), 0)
    block = jnp.ones((8, index.shape[1]), jnp.float32)
    for b in range(3):
        block = block * jnp.where(lax.shift_right_logical(row, b) & 1 == 1, bit_sign(index, b), 1.0)
    blocks = [block]
    for b in range(3, bits):
        factor = bit_sign(index, b)
        blocks = blocks + [block * factor for block in blocks]
    return jnp.concatenate(blocks, axis=0)


def answer_kernel(message, mine, theirs, left, right, signs):
    core = lax.shift_right_logical(lax.axis_index("all"), 2) & 1
    wanted = message[pl.ds(CHUNK - 1, CHIPS, stride=CHUNK), :]
    wanted = jnp.concatenate([wanted, pltpu.roll(wanted, LANES - HALVES * SLOTS, 1)], axis=0)
    wanted = wanted.T[: HALVES * SLOTS, :].astype(jnp.int32)
    factors = []
    for n in range(HALVES * SLOTS):
        index = wanted[n : n + 1, :]
        cut = slice(n * LANES, (n + 1) * LANES)
        table = sign_table(index & (LANES - 1), 7).astype(jnp.bfloat16)
        right[:LANES, cut] = table
        right[LANES:, cut] = table
        owner = lax.shift_right_logical(index, 14)
        chip = lax.shift_right_logical(owner, 3) * 4 + (owner & 3)
        signs[:, cut] = sign_table(chip, 6)
        factor = bit_sign(owner & (core * 4), 2)
        for b in range(6):
            if FIRST >> b & 1:
                factor = factor * bit_sign(chip, b)
        factors.append(factor)
    for half in range(HALVES):
        for pair in range(CHIPS // 2):
            tile = jnp.concatenate(
                [message[pl.ds(j * CHUNK + half * COLS, COLS), :] for j in (2 * pair, 2 * pair + 1)], axis=0
            )
            high, low = split(tile)
            left[half, pl.ds(pair * 16, 16), :LANES] = high
            left[half, pl.ds(pair * 16, 16), LANES:] = low
    answers = []
    width = 256
    for half in range(HALVES):
        for n in range(PICKS // width):
            cut = slice(half * PICKS + n * width, half * PICKS + (n + 1) * width)
            total = jnp.zeros((COLS, width), jnp.float32)
            for m in range(2):
                part = jnp.dot(
                    left[half, m * 256 : (m + 1) * 256, :], right[:, cut], preferred_element_type=jnp.float32
                )
                for j in range(32):
                    total = total + part[j * COLS : (j + 1) * COLS, :] * signs[m * 32 + j : m * 32 + j + 1, cut]
            answers += [total[:, :LANES], total[:, LANES:]]
    answers = [answer * factor for answer, factor in zip(answers, factors)]
    answers = jnp.concatenate(answers, axis=0).T
    mine[...] = answers[:CHIPS, :]
    theirs[...] = answers[CHIPS:, :]


def finish_kernel(reply, slots, sketch_hbm, gram_hbm, sketch, gram, sent):
    count = HALVES * SLOTS
    place = slots[...]
    hot = one_hot(lax.shift_right_logical(place, 4), CHIPS).astype(jnp.bfloat16)
    answers = jnp.concatenate([part.astype(jnp.float32) for part in split(reply[...])], axis=0)
    parts = jnp.dot(
        answers.T.astype(jnp.bfloat16), jnp.concatenate([hot, hot], axis=0), preferred_element_type=jnp.float32
    )
    place = place & (count - 1)
    total = jnp.zeros((COLS, PICKS), jnp.float32)
    for n in range(count):
        total = total + jnp.where(place == n, parts[n * COLS : (n + 1) * COLS, :], 0.0)
    sketch[...] = total
    first = pltpu.make_async_copy(sketch, sketch_hbm, sent.at[0])
    first.start()
    products = []
    for a in range(COLS):
        product = total * total[a : a + 1, :]
        products.append(sum(product[:, t * LANES : (t + 1) * LANES] for t in range(SLOTS)))
    products = jnp.concatenate(products + [jnp.zeros((LANES - COLS * COLS, LANES), jnp.float32)], axis=0)
    products = jnp.sum(products.T, axis=0, keepdims=True) * (1.0 / PICKS)
    gram[...] = products[:, : COLS * COLS]
    second = pltpu.make_async_copy(gram, gram_hbm, sent.at[1])
    second.start()
    first.wait()
    second.wait()


def on_device(matrix, flips, owners, offsets):
    f32, i32 = jnp.float32, jnp.int32
    params = pltpu.CompilerParams(vmem_limit_bytes=32 * 2**20)
    owners = owners.reshape(1, PICKS)
    offsets = offsets.reshape(1, PICKS)
    owners_other = other_core(owners)
    offsets_other = other_core(offsets)
    message_shape = jax.ShapeDtypeStruct((CHIPS * CHUNK, LANES), f32)
    message, own, slots = pl.pallas_call(
        send_kernel,
        name="transform_sections",
        out_shape=(
            message_shape,
            jax.ShapeDtypeStruct((CHIPS, LANES), f32),
            jax.ShapeDtypeStruct((1, PICKS), i32),
        ),
        in_specs=[HBM] * 4,
        out_specs=(VMEM, VMEM, VMEM),
        scratch_shapes=[
            pltpu.VMEM((COLS, LANES * LANES), f32),
            pltpu.VMEM((LANES, LANES), i32),
            pltpu.VMEM((1, PICKS), i32),
            pltpu.VMEM((1, PICKS), i32),
            pltpu.VMEM((LANES, COLS, LANES), f32),
            pltpu.SemaphoreType.DMA((3 + PIECES,)),
        ],
        compiler_params=params,
        cost_estimate=pl.CostEstimate(flops=2**22, bytes_accessed=4 * 2**20, transcendentals=0),
    )(
        *(
            pltpu.with_memory_space_constraint(operand, pltpu.HBM)
            for operand in (matrix, flips.reshape(LANES, LANES), owners, offsets)
        )
    )
    message = pl.pallas_call(
        ask_kernel,
        name="other_requests",
        out_shape=message_shape,
        in_specs=[VMEM] * 4,
        out_specs=VMEM,
        input_output_aliases={0: 0},
        compiler_params=params,
    )(message, own, owners_other, offsets_other)
    message = exchange(message)
    half_shape = jax.ShapeDtypeStruct((CHIPS, LANES), f32)
    mine, theirs = pl.pallas_call(
        answer_kernel,
        name="answer",
        out_shape=(half_shape, half_shape),
        in_specs=[VMEM],
        out_specs=(VMEM, VMEM),
        scratch_shapes=[
            pltpu.VMEM((HALVES, CHIPS * COLS, 2 * LANES), jnp.bfloat16),
            pltpu.VMEM((2 * LANES, HALVES * PICKS), jnp.bfloat16),
            pltpu.VMEM((CHIPS, HALVES * PICKS), f32),
        ],
        compiler_params=params,
    )(message)
    reply = exchange(mine + other_core(theirs))
    sketch, gram = pl.pallas_call(
        finish_kernel,
        name="finish",
        out_shape=(jax.ShapeDtypeStruct((COLS, PICKS), f32), jax.ShapeDtypeStruct((1, COLS * COLS), f32)),
        in_specs=[VMEM] * 2,
        out_specs=(HBM, HBM),
        scratch_shapes=[
            pltpu.VMEM((COLS, PICKS), f32),
            pltpu.VMEM((1, COLS * COLS), f32),
            pltpu.SemaphoreType.DMA((2,)),
        ],
        compiler_params=params,
    )(reply, slots)
    return sketch, gram.reshape(COLS * COLS, 1)


def solution(mesh):
    flat = Mesh(mesh.devices.reshape(-1), ("all",))
    in_specs = (P(None, "all"), P("all"), P("all", None), P("all"))
    out_specs = (P(None, "all"), P(None, "all"))
    return jax.shard_map(on_device, mesh=flat, in_specs=in_specs, out_specs=out_specs, check_vma=False)
```

```python
import math

import jax
import jax.numpy as jnp
from jax import lax
from jax.experimental import pallas as pl
from jax.experimental.pallas import tpu as pltpu
from jax.sharding import Mesh
from jax.sharding import PartitionSpec as P

LANES = 128
CHIPS = 64
HALVES = 2
SLOTS = 8
COLS = 8
CHUNK = HALVES * COLS + 1
PICKS = LANES * SLOTS
PIECES = 4
FIRST = 46
VMEM = pl.BlockSpec(memory_space=pltpu.VMEM)
HBM = pl.BlockSpec(memory_space=pltpu.HBM)


def device(chip, core):
    return (chip >> 2) * 8 + core * 4 + (chip & 3)


def exchange(rows):
    groups = [[device(j ^ FIRST, core) for j in range(CHIPS)] for core in range(2)]
    parts = rows.reshape(CHIPS, 1, -1)
    parts = lax.all_to_all(parts, "all", split_axis=0, concat_axis=0, tiled=True, axis_index_groups=groups)
    return parts.reshape(rows.shape)


def other_core(value):
    return lax.ppermute(value, "all", [(i, i ^ 4) for i in range(2 * CHIPS)])


def walsh(tiles):
    span = 1
    while span < len(tiles):
        out = list(tiles)
        for i in range(len(tiles)):
            if not i & span:
                out[i] = tiles[i] + tiles[i | span]
                out[i | span] = tiles[i] - tiles[i | span]
        tiles = out
        span *= 2
    return tiles


def one_hot(index, count):
    rows = lax.broadcasted_iota(jnp.int32, (count, index.shape[1]), 0)
    return (rows == index).astype(jnp.float32)


def split(values):
    high = values.astype(jnp.bfloat16)
    return high, (values - high.astype(jnp.float32)).astype(jnp.bfloat16)


def requests(place, owner):
    section = lax.shift_right_logical(place, 7)
    part = lax.shift_right_logical(section, 1) ^ FIRST
    mask = lax.broadcasted_iota(jnp.int32, (LANES, PICKS), 0) == (section & 1) * CHIPS + part
    hot = jnp.where(mask, 1.0, 0.0)
    first = lax.broadcasted_iota(jnp.int32, (2 * LANES, LANES), 0)
    second = lax.broadcasted_iota(jnp.int32, (2 * LANES, LANES), 1)
    table = jnp.where((first < second) | (first >= LANES), 1.0, 0.0).astype(jnp.bfloat16)
    earlier = jnp.zeros((LANES, LANES), jnp.float32)
    ranks = []
    for t in range(SLOTS):
        cut = slice(t * LANES, (t + 1) * LANES)
        some = hot[:, cut]
        before = jnp.concatenate([some, earlier], axis=1).astype(jnp.bfloat16)
        count = jnp.dot(before, table, preferred_element_type=jnp.float32)
        ranks.append(jnp.sum(jnp.where(mask[:, cut], count, 0.0), axis=0, keepdims=True))
        earlier = earlier + some
    rank = jnp.concatenate(ranks, axis=1).astype(jnp.int32)
    slot = lax.broadcasted_iota(jnp.int32, (SLOTS, PICKS), 0) == rank
    low = (place & (LANES - 1)).astype(jnp.float32)
    wanted = jnp.concatenate(
        [jnp.where(slot, owner.astype(jnp.float32), 0.0), jnp.where(slot, low, 0.0)], axis=0
    )
    found = lax.dot_general(
        wanted.astype(jnp.bfloat16),
        hot.astype(jnp.bfloat16),
        (((1,), (1,)), ((), ())),
        preferred_element_type=jnp.float32,
    )
    column = lax.broadcasted_iota(jnp.int32, (SLOTS, LANES), 1)
    section_of = (((column & (CHIPS - 1)) ^ FIRST) * 2 + lax.shift_right_logical(column, 6)).astype(jnp.float32)
    rows = found[:SLOTS] * float(LANES * LANES) + section_of * float(LANES) + found[SLOTS:]
    return rank, jnp.concatenate([rows, pltpu.roll(rows, CHIPS, 1)], axis=0)


def send_kernel(
    matrix_hbm, flips_hbm, owners_hbm, offsets_hbm, message, owners, offsets, matrix, flips, mid, arrived
):
    copies = [
        pltpu.make_async_copy(source, target, arrived.at[i])
        for i, (source, target) in enumerate(
            ((flips_hbm, flips), (owners_hbm, owners), (offsets_hbm, offsets))
        )
    ]
    width = matrix.shape[1] // PIECES
    for p in range(PIECES):
        cut = pl.ds(p * width, width)
        copies.append(pltpu.make_async_copy(matrix_hbm.at[:, cut], matrix.at[:, cut], arrived.at[3 + p]))
    for copy in copies:
        copy.start()
    scale = 1.0 / math.sqrt(float(LANES) ** 3)
    copies[0].wait()
    signs = jnp.where(flips[...] == 1, scale, -scale)
    for i in range(16):
        if i * PIECES % 16 == 0:
            copies[3 + i * PIECES // 16].wait()
        tiles = []
        for f in range(i * 8, i * 8 + 8):
            tiles.append(matrix[:, f * LANES : (f + 1) * LANES] * signs[f : f + 1, :])
        for j, tile in enumerate(walsh(tiles)):
            mid[i * 8 + j] = tile
    for j in range(8):
        for i, tile in enumerate(walsh([mid[i * 8 + j] for i in range(16)])):
            section = i * 8 + j
            row = ((section >> 1) ^ FIRST) * CHUNK + (section & 1) * COLS
            message[pl.ds(row, COLS), :] = tile
    copies[1].wait()
    copies[2].wait()


def ask_kernel(_, owners, offsets, owners_other, offsets_other, message, slots):
    place = offsets[...]
    rank, rows = requests(place, owners[...])
    _, rows_other = requests(offsets_other[...], owners_other[...])
    rest = jnp.zeros((LANES - 2 * HALVES * SLOTS, LANES), jnp.float32)
    rows = jnp.concatenate([rows, rows_other, rest], axis=0).T
    message[pl.ds(CHUNK - 1, CHIPS, stride=CHUNK), :] = rows[:CHIPS]
    section = lax.shift_right_logical(place, 7)
    part = lax.shift_right_logical(section, 1) ^ FIRST
    slot = (section & 1) * SLOTS + rank
    slots[...] = part * (HALVES * SLOTS) + (slot & 1) * SLOTS + lax.shift_right_logical(slot, 1)


def bit_sign(index, bit):
    return 1.0 - 2.0 * (lax.shift_right_logical(index, bit) & 1).astype(jnp.float32)


def sign_table(index, bits):
    row = lax.broadcasted_iota(jnp.int32, (8, index.shape[1]), 0)
    block = jnp.ones((8, index.shape[1]), jnp.float32)
    for b in range(3):
        block = block * jnp.where(lax.shift_right_logical(row, b) & 1 == 1, bit_sign(index, b), 1.0)
    blocks = [block]
    for b in range(3, bits):
        factor = bit_sign(index, b)
        blocks = blocks + [block * factor for block in blocks]
    return jnp.concatenate(blocks, axis=0)


def answer(message, kind, left, reply, right, signs):
    core = lax.shift_right_logical(lax.axis_index("all"), 2) & 1
    count = HALVES * SLOTS
    wanted = message[pl.ds(CHUNK - 1, CHIPS, stride=CHUNK), :]
    even, odd = [(LANES - kind * count - n) % LANES for n in range(2)]
    wanted = jnp.concatenate([pltpu.roll(wanted, even, 1) if even else wanted, pltpu.roll(wanted, odd, 1)], axis=0)
    wanted = wanted.T[:count, :].astype(jnp.int32)
    factors = []
    for n in range(count // 2):
        index = wanted[2 * n : 2 * n + 1, :]
        cut = slice(n * LANES, (n + 1) * LANES)
        table = sign_table(index & (LANES - 1), 7).astype(jnp.bfloat16)
        right[:LANES, cut] = table
        right[LANES:, cut] = table
        owner = lax.shift_right_logical(index, 14)
        chip = lax.shift_right_logical(owner, 3) * 4 + (owner & 3)
        signs[:, cut] = sign_table(chip, 6)
        factor = bit_sign(owner & (core * 4), 2)
        for b in range(6):
            if FIRST >> b & 1:
                factor = factor * bit_sign(chip, b)
        factors.append(factor)
    answers = []
    width = 256
    for half in range(HALVES):
        for n in range(PICKS // 2 // width):
            cut = slice(half * PICKS // 2 + n * width, half * PICKS // 2 + (n + 1) * width)
            total = jnp.zeros((COLS, width), jnp.float32)
            for m in range(2):
                part = jnp.dot(
                    left[half, m * 256 : (m + 1) * 256, :], right[:, cut], preferred_element_type=jnp.float32
                )
                for j in range(32):
                    total = total + part[j * COLS : (j + 1) * COLS, :] * signs[m * 32 + j : m * 32 + j + 1, cut]
            answers += [total[:, :LANES], total[:, LANES:]]
    answers = jnp.concatenate([answer * factor for answer, factor in zip(answers, factors)], axis=0)
    reply[...] = jnp.concatenate([answers, pltpu.roll(answers, CHIPS, 1)], axis=0).T[:CHIPS]


def answer_other_kernel(message, reply, left, right, signs):
    for half in range(HALVES):
        for pair in range(CHIPS // 2):
            tile = jnp.concatenate(
                [message[pl.ds(j * CHUNK + half * COLS, COLS), :] for j in (2 * pair, 2 * pair + 1)], axis=0
            )
            high, low = split(tile)
            left[half, pl.ds(pair * 16, 16), :LANES] = high
            left[half, pl.ds(pair * 16, 16), LANES:] = low
    answer(message, 1, left, reply, right, signs)


def answer_own_kernel(message, left, reply, right, signs):
    answer(message, 0, left, reply, right, signs)


def finish_kernel(reply, slots, sketch_hbm, gram_hbm, sketch, gram, sent):
    count = HALVES * SLOTS
    place = slots[...]
    hot = one_hot(lax.shift_right_logical(place, 4), CHIPS).astype(jnp.bfloat16)
    answers = jnp.concatenate([part.astype(jnp.float32) for part in split(reply[...])], axis=0)
    parts = jnp.dot(
        answers.T.astype(jnp.bfloat16), jnp.concatenate([hot, hot], axis=0), preferred_element_type=jnp.float32
    )
    place = place & (count - 1)
    total = jnp.zeros((COLS, PICKS), jnp.float32)
    for n in range(count):
        total = total + jnp.where(place == n, parts[n * COLS : (n + 1) * COLS, :], 0.0)
    sketch[...] = total
    first = pltpu.make_async_copy(sketch, sketch_hbm, sent.at[0])
    first.start()
    products = []
    for a in range(COLS):
        product = total * total[a : a + 1, :]
        products.append(sum(product[:, t * LANES : (t + 1) * LANES] for t in range(SLOTS)))
    products = jnp.concatenate(products + [jnp.zeros((LANES - COLS * COLS, LANES), jnp.float32)], axis=0)
    products = jnp.sum(products.T, axis=0, keepdims=True) * (1.0 / PICKS)
    gram[...] = products[:, : COLS * COLS]
    second = pltpu.make_async_copy(gram, gram_hbm, sent.at[1])
    second.start()
    first.wait()
    second.wait()


def on_device(matrix, flips, owners, offsets):
    f32, i32 = jnp.float32, jnp.int32
    params = pltpu.CompilerParams(vmem_limit_bytes=32 * 2**20)
    owners = owners.reshape(1, PICKS)
    offsets = offsets.reshape(1, PICKS)
    owners_other = other_core(owners)
    offsets_other = other_core(offsets)
    message_shape = jax.ShapeDtypeStruct((CHIPS * CHUNK, LANES), f32)
    picks_shape = jax.ShapeDtypeStruct((1, PICKS), i32)
    message, owners, offsets = pl.pallas_call(
        send_kernel,
        name="transform_sections",
        out_shape=(message_shape, picks_shape, picks_shape),
        in_specs=[HBM] * 4,
        out_specs=(VMEM, VMEM, VMEM),
        scratch_shapes=[
            pltpu.VMEM((COLS, LANES * LANES), f32),
            pltpu.VMEM((LANES, LANES), i32),
            pltpu.VMEM((LANES, COLS, LANES), f32),
            pltpu.SemaphoreType.DMA((3 + PIECES,)),
        ],
        compiler_params=params,
        cost_estimate=pl.CostEstimate(flops=2**22, bytes_accessed=4 * 2**20, transcendentals=0),
    )(
        *(
            pltpu.with_memory_space_constraint(operand, pltpu.HBM)
            for operand in (matrix, flips.reshape(LANES, LANES), owners, offsets)
        )
    )
    message, slots = pl.pallas_call(
        ask_kernel,
        name="requests",
        out_shape=(message_shape, picks_shape),
        in_specs=[VMEM] * 5,
        out_specs=(VMEM, VMEM),
        input_output_aliases={0: 0},
        compiler_params=params,
    )(message, owners, offsets, owners_other, offsets_other)
    message = exchange(message)
    reply_shape = jax.ShapeDtypeStruct((CHIPS, LANES), f32)
    tables = [pltpu.VMEM((2 * LANES, PICKS), jnp.bfloat16), pltpu.VMEM((CHIPS, PICKS), f32)]
    theirs, left = pl.pallas_call(
        answer_other_kernel,
        name="answer_other",
        out_shape=(reply_shape, jax.ShapeDtypeStruct((HALVES, CHIPS * COLS, 2 * LANES), jnp.bfloat16)),
        in_specs=[VMEM],
        out_specs=(VMEM, VMEM),
        scratch_shapes=tables,
        compiler_params=params,
    )(message)
    theirs = other_core(theirs)
    mine = pl.pallas_call(
        answer_own_kernel,
        name="answer_own",
        out_shape=reply_shape,
        in_specs=[VMEM, VMEM],
        out_specs=VMEM,
        scratch_shapes=tables,
        compiler_params=params,
        cost_estimate=pl.CostEstimate(flops=2**28, bytes_accessed=2**21, transcendentals=0),
    )(message, left)
    reply = exchange(mine + theirs)
    sketch, gram = pl.pallas_call(
        finish_kernel,
        name="finish",
        out_shape=(jax.ShapeDtypeStruct((COLS, PICKS), f32), jax.ShapeDtypeStruct((1, COLS * COLS), f32)),
        in_specs=[VMEM] * 2,
        out_specs=(HBM, HBM),
        scratch_shapes=[
            pltpu.VMEM((COLS, PICKS), f32),
            pltpu.VMEM((1, COLS * COLS), f32),
            pltpu.SemaphoreType.DMA((2,)),
        ],
        compiler_params=params,
    )(reply, slots)
    return sketch, gram.reshape(COLS * COLS, 1)


def solution(mesh):
    flat = Mesh(mesh.devices.reshape(-1), ("all",))
    in_specs = (P(None, "all"), P("all"), P("all", None), P("all"))
    out_specs = (P(None, "all"), P(None, "all"))
    return jax.shard_map(on_device, mesh=flat, in_specs=in_specs, out_specs=out_specs, check_vma=False)
```

```python
import math

import jax
import jax.numpy as jnp
from jax import lax
from jax.experimental import pallas as pl
from jax.experimental.pallas import tpu as pltpu
from jax.sharding import Mesh
from jax.sharding import PartitionSpec as P

LANES = 128
CHIPS = 64
HALVES = 2
SLOTS = 8
COLS = 8
CHUNK = HALVES * COLS + 1
PICKS = LANES * SLOTS
PIECES = 4
FIRST = 46
FIRST_BACK = 42
VMEM = pl.BlockSpec(memory_space=pltpu.VMEM)
HBM = pl.BlockSpec(memory_space=pltpu.HBM)


def device(chip, core):
    return (chip >> 2) * 8 + core * 4 + (chip & 3)


def exchange(rows, first):
    groups = [[device(j ^ first, core) for j in range(CHIPS)] for core in range(2)]
    parts = rows.reshape(CHIPS, 1, -1)
    parts = lax.all_to_all(parts, "all", split_axis=0, concat_axis=0, tiled=True, axis_index_groups=groups)
    return parts.reshape(rows.shape)


def other_core(value):
    return lax.ppermute(value, "all", [(i, i ^ 4) for i in range(2 * CHIPS)])


def walsh(tiles):
    span = 1
    while span < len(tiles):
        out = list(tiles)
        for i in range(len(tiles)):
            if not i & span:
                out[i] = tiles[i] + tiles[i | span]
                out[i | span] = tiles[i] - tiles[i | span]
        tiles = out
        span *= 2
    return tiles


def one_hot(index, count):
    rows = lax.broadcasted_iota(jnp.int32, (count, index.shape[1]), 0)
    return (rows == index).astype(jnp.float32)


def split(values):
    high = values.astype(jnp.bfloat16)
    return high, (values - high.astype(jnp.float32)).astype(jnp.bfloat16)


def requests(place, owner):
    section = lax.shift_right_logical(place, 7)
    part = lax.shift_right_logical(section, 1) ^ FIRST
    mask = lax.broadcasted_iota(jnp.int32, (LANES, PICKS), 0) == (section & 1) * CHIPS + part
    hot = jnp.where(mask, 1.0, 0.0)
    first = lax.broadcasted_iota(jnp.int32, (2 * LANES, LANES), 0)
    second = lax.broadcasted_iota(jnp.int32, (2 * LANES, LANES), 1)
    table = jnp.where((first < second) | (first >= LANES), 1.0, 0.0).astype(jnp.bfloat16)
    earlier = jnp.zeros((LANES, LANES), jnp.float32)
    ranks = []
    for t in range(SLOTS):
        cut = slice(t * LANES, (t + 1) * LANES)
        some = hot[:, cut]
        before = jnp.concatenate([some, earlier], axis=1).astype(jnp.bfloat16)
        count = jnp.dot(before, table, preferred_element_type=jnp.float32)
        ranks.append(jnp.sum(jnp.where(mask[:, cut], count, 0.0), axis=0, keepdims=True))
        earlier = earlier + some
    rank = jnp.concatenate(ranks, axis=1).astype(jnp.int32)
    slot = lax.broadcasted_iota(jnp.int32, (SLOTS, PICKS), 0) == rank
    low = (place & (LANES - 1)).astype(jnp.float32)
    wanted = jnp.concatenate(
        [jnp.where(slot, owner.astype(jnp.float32), 0.0), jnp.where(slot, low, 0.0)], axis=0
    )
    found = lax.dot_general(
        wanted.astype(jnp.bfloat16),
        hot.astype(jnp.bfloat16),
        (((1,), (1,)), ((), ())),
        preferred_element_type=jnp.float32,
    )
    column = lax.broadcasted_iota(jnp.int32, (SLOTS, LANES), 1)
    section_of = (((column & (CHIPS - 1)) ^ FIRST) * 2 + lax.shift_right_logical(column, 6)).astype(jnp.float32)
    rows = found[:SLOTS] * float(LANES * LANES) + section_of * float(LANES) + found[SLOTS:]
    return rank, jnp.concatenate([rows, pltpu.roll(rows, CHIPS, 1)], axis=0)


def send_kernel(
    matrix_hbm, flips_hbm, owners_hbm, offsets_hbm, message, owners, offsets, matrix, flips, mid, arrived
):
    copies = [
        pltpu.make_async_copy(source, target, arrived.at[i])
        for i, (source, target) in enumerate(
            ((flips_hbm, flips), (owners_hbm, owners), (offsets_hbm, offsets))
        )
    ]
    width = matrix.shape[1] // PIECES
    for p in range(PIECES):
        cut = pl.ds(p * width, width)
        copies.append(pltpu.make_async_copy(matrix_hbm.at[:, cut], matrix.at[:, cut], arrived.at[3 + p]))
    for copy in copies:
        copy.start()
    scale = 1.0 / math.sqrt(float(LANES) ** 3)
    copies[0].wait()
    signs = jnp.where(flips[...] == 1, scale, -scale)
    for i in range(16):
        if i * PIECES % 16 == 0:
            copies[3 + i * PIECES // 16].wait()
        tiles = []
        for f in range(i * 8, i * 8 + 8):
            tiles.append(matrix[:, f * LANES : (f + 1) * LANES] * signs[f : f + 1, :])
        for j, tile in enumerate(walsh(tiles)):
            mid[i * 8 + j] = tile
    for j in range(8):
        for i, tile in enumerate(walsh([mid[i * 8 + j] for i in range(16)])):
            section = i * 8 + j
            row = ((section >> 1) ^ FIRST) * CHUNK + (section & 1) * COLS
            message[pl.ds(row, COLS), :] = tile
    copies[1].wait()
    copies[2].wait()


def ask_kernel(_, owners, offsets, owners_other, offsets_other, message, slots):
    place = offsets[...]
    rank, rows = requests(place, owners[...])
    _, rows_other = requests(offsets_other[...], owners_other[...])
    rest = jnp.zeros((LANES - 2 * HALVES * SLOTS, LANES), jnp.float32)
    rows = jnp.concatenate([rows, rows_other, rest], axis=0).T
    message[pl.ds(CHUNK - 1, CHIPS, stride=CHUNK), :] = rows[:CHIPS]
    section = lax.shift_right_logical(place, 7)
    part = lax.shift_right_logical(section, 1) ^ FIRST_BACK
    slot = (section & 1) * SLOTS + rank
    slots[...] = part * (HALVES * SLOTS) + (slot & 1) * SLOTS + lax.shift_right_logical(slot, 1)


def bit_sign(index, bit):
    return 1.0 - 2.0 * (lax.shift_right_logical(index, bit) & 1).astype(jnp.float32)


def sign_table(index, bits):
    row = lax.broadcasted_iota(jnp.int32, (8, index.shape[1]), 0)
    block = jnp.ones((8, index.shape[1]), jnp.float32)
    for b in range(3):
        block = block * jnp.where(lax.shift_right_logical(row, b) & 1 == 1, bit_sign(index, b), 1.0)
    blocks = [block]
    for b in range(3, bits):
        factor = bit_sign(index, b)
        blocks = blocks + [block * factor for block in blocks]
    return jnp.concatenate(blocks, axis=0)


def reorder(rows, flip):
    tiles = [rows[8 * i : 8 * i + 8] for i in range(rows.shape[0] // 8)]
    tiles = [tiles[i ^ (flip >> 3)] for i in range(len(tiles))]
    return jnp.concatenate([pltpu.roll(tile, 4, 0) if flip & 4 else tile for tile in tiles], axis=0)


def answer(message, kind, left, reply, right, signs):
    core = lax.shift_right_logical(lax.axis_index("all"), 2) & 1
    count = HALVES * SLOTS
    wanted = reorder(message[pl.ds(CHUNK - 1, CHIPS, stride=CHUNK), :], FIRST ^ FIRST_BACK)
    even, odd = [(LANES - kind * count - n) % LANES for n in range(2)]
    wanted = jnp.concatenate([pltpu.roll(wanted, even, 1) if even else wanted, pltpu.roll(wanted, odd, 1)], axis=0)
    wanted = wanted.T[:count, :].astype(jnp.int32)
    factors = []
    for n in range(count // 2):
        index = wanted[2 * n : 2 * n + 1, :]
        cut = slice(n * LANES, (n + 1) * LANES)
        table = sign_table(index & (LANES - 1), 7).astype(jnp.bfloat16)
        right[:LANES, cut] = table
        right[LANES:, cut] = table
        owner = lax.shift_right_logical(index, 14)
        chip = lax.shift_right_logical(owner, 3) * 4 + (owner & 3)
        signs[:, cut] = sign_table(chip, 6)
        factor = bit_sign(owner & (core * 4), 2)
        for b in range(6):
            if FIRST >> b & 1:
                factor = factor * bit_sign(chip, b)
        factors.append(factor)
    answers = []
    width = 256
    for half in range(HALVES):
        for n in range(PICKS // 2 // width):
            cut = slice(half * PICKS // 2 + n * width, half * PICKS // 2 + (n + 1) * width)
            total = jnp.zeros((COLS, width), jnp.float32)
            for m in range(2):
                part = jnp.dot(
                    left[half, m * 256 : (m + 1) * 256, :], right[:, cut], preferred_element_type=jnp.float32
                )
                for j in range(32):
                    total = total + part[j * COLS : (j + 1) * COLS, :] * signs[m * 32 + j : m * 32 + j + 1, cut]
            answers += [total[:, :LANES], total[:, LANES:]]
    answers = jnp.concatenate([answer * factor for answer, factor in zip(answers, factors)], axis=0)
    reply[...] = jnp.concatenate([answers, pltpu.roll(answers, CHIPS, 1)], axis=0).T[:CHIPS]


def answer_other_kernel(message, reply, left, right, signs):
    for half in range(HALVES):
        for pair in range(CHIPS // 2):
            tile = jnp.concatenate(
                [message[pl.ds(j * CHUNK + half * COLS, COLS), :] for j in (2 * pair, 2 * pair + 1)], axis=0
            )
            high, low = split(tile)
            left[half, pl.ds(pair * 16, 16), :LANES] = high
            left[half, pl.ds(pair * 16, 16), LANES:] = low
    answer(message, 1, left, reply, right, signs)


def answer_own_kernel(message, left, reply, right, signs):
    answer(message, 0, left, reply, right, signs)


def finish_kernel(reply, slots, sketch_hbm, gram_hbm, sketch, gram, sent):
    count = HALVES * SLOTS
    place = slots[...]
    hot = one_hot(lax.shift_right_logical(place, 4), CHIPS).astype(jnp.bfloat16)
    answers = jnp.concatenate([part.astype(jnp.float32) for part in split(reply[...])], axis=0)
    parts = jnp.dot(
        answers.T.astype(jnp.bfloat16), jnp.concatenate([hot, hot], axis=0), preferred_element_type=jnp.float32
    )
    place = place & (count - 1)
    total = jnp.zeros((COLS, PICKS), jnp.float32)
    for n in range(count):
        total = total + jnp.where(place == n, parts[n * COLS : (n + 1) * COLS, :], 0.0)
    sketch[...] = total
    first = pltpu.make_async_copy(sketch, sketch_hbm, sent.at[0])
    first.start()
    products = []
    for a in range(COLS):
        product = total * total[a : a + 1, :]
        products.append(sum(product[:, t * LANES : (t + 1) * LANES] for t in range(SLOTS)))
    products = jnp.concatenate(products + [jnp.zeros((LANES - COLS * COLS, LANES), jnp.float32)], axis=0)
    products = jnp.sum(products.T, axis=0, keepdims=True) * (1.0 / PICKS)
    gram[...] = products[:, : COLS * COLS]
    second = pltpu.make_async_copy(gram, gram_hbm, sent.at[1])
    second.start()
    first.wait()
    second.wait()


def on_device(matrix, flips, owners, offsets):
    f32, i32 = jnp.float32, jnp.int32
    params = pltpu.CompilerParams(vmem_limit_bytes=32 * 2**20)
    owners = owners.reshape(1, PICKS)
    offsets = offsets.reshape(1, PICKS)
    owners_other = other_core(owners)
    offsets_other = other_core(offsets)
    message_shape = jax.ShapeDtypeStruct((CHIPS * CHUNK, LANES), f32)
    picks_shape = jax.ShapeDtypeStruct((1, PICKS), i32)
    message, owners, offsets = pl.pallas_call(
        send_kernel,
        name="transform_sections",
        out_shape=(message_shape, picks_shape, picks_shape),
        in_specs=[HBM] * 4,
        out_specs=(VMEM, VMEM, VMEM),
        scratch_shapes=[
            pltpu.VMEM((COLS, LANES * LANES), f32),
            pltpu.VMEM((LANES, LANES), i32),
            pltpu.VMEM((LANES, COLS, LANES), f32),
            pltpu.SemaphoreType.DMA((3 + PIECES,)),
        ],
        compiler_params=params,
        cost_estimate=pl.CostEstimate(flops=2**22, bytes_accessed=4 * 2**20, transcendentals=0),
    )(
        *(
            pltpu.with_memory_space_constraint(operand, pltpu.HBM)
            for operand in (matrix, flips.reshape(LANES, LANES), owners, offsets)
        )
    )
    message, slots = pl.pallas_call(
        ask_kernel,
        name="requests",
        out_shape=(message_shape, picks_shape),
        in_specs=[VMEM] * 5,
        out_specs=(VMEM, VMEM),
        input_output_aliases={0: 0},
        compiler_params=params,
    )(message, owners, offsets, owners_other, offsets_other)
    message = exchange(message, FIRST)
    reply_shape = jax.ShapeDtypeStruct((CHIPS, LANES), f32)
    tables = [pltpu.VMEM((2 * LANES, PICKS), jnp.bfloat16), pltpu.VMEM((CHIPS, PICKS), f32)]
    theirs, left = pl.pallas_call(
        answer_other_kernel,
        name="answer_other",
        out_shape=(reply_shape, jax.ShapeDtypeStruct((HALVES, CHIPS * COLS, 2 * LANES), jnp.bfloat16)),
        in_specs=[VMEM],
        out_specs=(VMEM, VMEM),
        scratch_shapes=tables,
        compiler_params=params,
    )(message)
    theirs = other_core(theirs)
    mine = pl.pallas_call(
        answer_own_kernel,
        name="answer_own",
        out_shape=reply_shape,
        in_specs=[VMEM, VMEM],
        out_specs=VMEM,
        scratch_shapes=tables,
        compiler_params=params,
        cost_estimate=pl.CostEstimate(flops=2**28, bytes_accessed=2**21, transcendentals=0),
    )(message, left)
    reply = exchange(mine + theirs, FIRST_BACK)
    sketch, gram = pl.pallas_call(
        finish_kernel,
        name="finish",
        out_shape=(jax.ShapeDtypeStruct((COLS, PICKS), f32), jax.ShapeDtypeStruct((1, COLS * COLS), f32)),
        in_specs=[VMEM] * 2,
        out_specs=(HBM, HBM),
        scratch_shapes=[
            pltpu.VMEM((COLS, PICKS), f32),
            pltpu.VMEM((1, COLS * COLS), f32),
            pltpu.SemaphoreType.DMA((2,)),
        ],
        compiler_params=params,
    )(reply, slots)
    return sketch, gram.reshape(COLS * COLS, 1)


def solution(mesh):
    flat = Mesh(mesh.devices.reshape(-1), ("all",))
    in_specs = (P(None, "all"), P("all"), P("all", None), P("all"))
    out_specs = (P(None, "all"), P(None, "all"))
    return jax.shard_map(on_device, mesh=flat, in_specs=in_specs, out_specs=out_specs, check_vma=False)
```

```python
import math

import jax
import jax.numpy as jnp
from jax import lax
from jax.experimental import pallas as pl
from jax.experimental.pallas import tpu as pltpu
from jax.sharding import Mesh
from jax.sharding import PartitionSpec as P

LANES = 128
CHIPS = 64
HALVES = 2
SLOTS = 8
COLS = 8
CHUNK = HALVES * COLS + 1
PICKS = LANES * SLOTS
PIECES = 4
FIRST = 46
FIRST_BACK = 42
VMEM = pl.BlockSpec(memory_space=pltpu.VMEM)
HBM = pl.BlockSpec(memory_space=pltpu.HBM)


def device(chip, core):
    return (chip >> 2) * 8 + core * 4 + (chip & 3)


def exchange(rows, first):
    groups = [[device(j ^ first, core) for j in range(CHIPS)] for core in range(2)]
    parts = rows.reshape(CHIPS, 1, -1)
    parts = lax.all_to_all(parts, "all", split_axis=0, concat_axis=0, tiled=True, axis_index_groups=groups)
    return parts.reshape(rows.shape)


def other_core(value):
    return lax.ppermute(value, "all", [(i, i ^ 4) for i in range(2 * CHIPS)])


def walsh(tiles):
    span = 1
    while span < len(tiles):
        out = list(tiles)
        for i in range(len(tiles)):
            if not i & span:
                out[i] = tiles[i] + tiles[i | span]
                out[i | span] = tiles[i] - tiles[i | span]
        tiles = out
        span *= 2
    return tiles


def one_hot(index, count):
    rows = lax.broadcasted_iota(jnp.int32, (count, index.shape[1]), 0)
    return (rows == index).astype(jnp.float32)


def split(values):
    high = values.astype(jnp.bfloat16)
    return high, (values - high.astype(jnp.float32)).astype(jnp.bfloat16)


def requests(place, owner):
    section = lax.shift_right_logical(place, 7)
    part = lax.shift_right_logical(section, 1) ^ FIRST
    mask = lax.broadcasted_iota(jnp.int32, (LANES, PICKS), 0) == (section & 1) * CHIPS + part
    hot = jnp.where(mask, 1.0, 0.0)
    first = lax.broadcasted_iota(jnp.int32, (2 * LANES, LANES), 0)
    second = lax.broadcasted_iota(jnp.int32, (2 * LANES, LANES), 1)
    table = jnp.where((first < second) | (first >= LANES), 1.0, 0.0).astype(jnp.bfloat16)
    earlier = jnp.zeros((LANES, LANES), jnp.float32)
    ranks = []
    for t in range(SLOTS):
        cut = slice(t * LANES, (t + 1) * LANES)
        some = hot[:, cut]
        before = jnp.concatenate([some, earlier], axis=1).astype(jnp.bfloat16)
        count = jnp.dot(before, table, preferred_element_type=jnp.float32)
        ranks.append(jnp.sum(jnp.where(mask[:, cut], count, 0.0), axis=0, keepdims=True))
        earlier = earlier + some
    rank = jnp.concatenate(ranks, axis=1).astype(jnp.int32)
    slot = lax.broadcasted_iota(jnp.int32, (SLOTS, PICKS), 0) == rank
    low = (place & (LANES - 1)).astype(jnp.float32)
    wanted = jnp.concatenate(
        [jnp.where(slot, owner.astype(jnp.float32), 0.0), jnp.where(slot, low, 0.0)], axis=0
    )
    found = lax.dot_general(
        wanted.astype(jnp.bfloat16),
        hot.astype(jnp.bfloat16),
        (((1,), (1,)), ((), ())),
        preferred_element_type=jnp.float32,
    )
    column = lax.broadcasted_iota(jnp.int32, (SLOTS, LANES), 1)
    section_of = (((column & (CHIPS - 1)) ^ FIRST) * 2 + lax.shift_right_logical(column, 6)).astype(jnp.float32)
    rows = found[:SLOTS] * float(LANES * LANES) + section_of * float(LANES) + found[SLOTS:]
    return rank, jnp.concatenate([rows, pltpu.roll(rows, CHIPS, 1)], axis=0)


def load_kernel(
    matrix_hbm, flips_hbm, owners_hbm, offsets_hbm, matrix, flips, own, slots, owners, offsets, arrived
):
    copies = [
        pltpu.make_async_copy(source, target, arrived.at[i])
        for i, (source, target) in enumerate(
            ((flips_hbm, flips), (owners_hbm, owners), (offsets_hbm, offsets))
        )
    ]
    width = matrix.shape[1] // PIECES
    for p in range(PIECES):
        cut = pl.ds(p * width, width)
        copies.append(pltpu.make_async_copy(matrix_hbm.at[:, cut], matrix.at[:, cut], arrived.at[3 + p]))
    for copy in copies:
        copy.start()
    copies[1].wait()
    copies[2].wait()
    place = offsets[...]
    rank, rows = requests(place, owners[...])
    own[...] = rows
    section = lax.shift_right_logical(place, 7)
    part = lax.shift_right_logical(section, 1) ^ FIRST_BACK
    slot = (section & 1) * SLOTS + rank
    slots[...] = part * (HALVES * SLOTS) + (slot & 1) * SLOTS + lax.shift_right_logical(slot, 1)
    for copy in [copies[0]] + copies[3:]:
        copy.wait()


def send_kernel(matrix, flips, own, owners, offsets, message, mid):
    _, rows = requests(offsets[...], owners[...])
    rest = jnp.zeros((LANES - 2 * HALVES * SLOTS, LANES), jnp.float32)
    rows = jnp.concatenate([own[...], rows, rest], axis=0).T
    message[pl.ds(CHUNK - 1, CHIPS, stride=CHUNK), :] = rows[:CHIPS]
    scale = 1.0 / math.sqrt(float(LANES) ** 3)
    signs = jnp.where(flips[...] == 1, scale, -scale)
    for i in range(16):
        tiles = []
        for f in range(i * 8, i * 8 + 8):
            tiles.append(matrix[:, f * LANES : (f + 1) * LANES] * signs[f : f + 1, :])
        for j, tile in enumerate(walsh(tiles)):
            mid[i * 8 + j] = tile
    for j in range(8):
        for i, tile in enumerate(walsh([mid[i * 8 + j] for i in range(16)])):
            section = i * 8 + j
            row = ((section >> 1) ^ FIRST) * CHUNK + (section & 1) * COLS
            message[pl.ds(row, COLS), :] = tile


def bit_sign(index, bit):
    return 1.0 - 2.0 * (lax.shift_right_logical(index, bit) & 1).astype(jnp.float32)


def sign_table(index, bits):
    row = lax.broadcasted_iota(jnp.int32, (8, index.shape[1]), 0)
    block = jnp.ones((8, index.shape[1]), jnp.float32)
    for b in range(3):
        block = block * jnp.where(lax.shift_right_logical(row, b) & 1 == 1, bit_sign(index, b), 1.0)
    blocks = [block]
    for b in range(3, bits):
        factor = bit_sign(index, b)
        blocks = blocks + [block * factor for block in blocks]
    return jnp.concatenate(blocks, axis=0)


def reorder(rows, flip):
    tiles = [rows[8 * i : 8 * i + 8] for i in range(rows.shape[0] // 8)]
    tiles = [tiles[i ^ (flip >> 3)] for i in range(len(tiles))]
    return jnp.concatenate([pltpu.roll(tile, 4, 0) if flip & 4 else tile for tile in tiles], axis=0)


def answer(message, kind, left, reply, right, signs):
    core = lax.shift_right_logical(lax.axis_index("all"), 2) & 1
    count = HALVES * SLOTS
    wanted = reorder(message[pl.ds(CHUNK - 1, CHIPS, stride=CHUNK), :], FIRST ^ FIRST_BACK)
    even, odd = [(LANES - kind * count - n) % LANES for n in range(2)]
    wanted = jnp.concatenate([pltpu.roll(wanted, even, 1) if even else wanted, pltpu.roll(wanted, odd, 1)], axis=0)
    wanted = wanted.T[:count, :].astype(jnp.int32)
    factors = []
    for n in range(count // 2):
        index = wanted[2 * n : 2 * n + 1, :]
        cut = slice(n * LANES, (n + 1) * LANES)
        table = sign_table(index & (LANES - 1), 7).astype(jnp.bfloat16)
        right[:LANES, cut] = table
        right[LANES:, cut] = table
        owner = lax.shift_right_logical(index, 14)
        chip = lax.shift_right_logical(owner, 3) * 4 + (owner & 3)
        signs[:, cut] = sign_table(chip, 6)
        factor = bit_sign(owner & (core * 4), 2)
        for b in range(6):
            if FIRST >> b & 1:
                factor = factor * bit_sign(chip, b)
        factors.append(factor)
    answers = []
    width = 256
    for half in range(HALVES):
        for n in range(PICKS // 2 // width):
            cut = slice(half * PICKS // 2 + n * width, half * PICKS // 2 + (n + 1) * width)
            total = jnp.zeros((COLS, width), jnp.float32)
            for m in range(2):
                part = jnp.dot(
                    left[half, m * 256 : (m + 1) * 256, :], right[:, cut], preferred_element_type=jnp.float32
                )
                for j in range(32):
                    total = total + part[j * COLS : (j + 1) * COLS, :] * signs[m * 32 + j : m * 32 + j + 1, cut]
            answers += [total[:, :LANES], total[:, LANES:]]
    answers = jnp.concatenate([answer * factor for answer, factor in zip(answers, factors)], axis=0)
    reply[...] = jnp.concatenate([answers, pltpu.roll(answers, CHIPS, 1)], axis=0).T[:CHIPS]


def answer_other_kernel(message, reply, left, right, signs):
    for half in range(HALVES):
        for pair in range(CHIPS // 2):
            tile = jnp.concatenate(
                [message[pl.ds(j * CHUNK + half * COLS, COLS), :] for j in (2 * pair, 2 * pair + 1)], axis=0
            )
            high, low = split(tile)
            left[half, pl.ds(pair * 16, 16), :LANES] = high
            left[half, pl.ds(pair * 16, 16), LANES:] = low
    answer(message, 1, left, reply, right, signs)


def answer_own_kernel(message, left, reply, right, signs):
    answer(message, 0, left, reply, right, signs)


def finish_kernel(reply, slots, sketch_hbm, gram_hbm, sketch, gram, sent):
    count = HALVES * SLOTS
    place = slots[...]
    hot = one_hot(lax.shift_right_logical(place, 4), CHIPS).astype(jnp.bfloat16)
    answers = jnp.concatenate([part.astype(jnp.float32) for part in split(reply[...])], axis=0)
    parts = jnp.dot(
        answers.T.astype(jnp.bfloat16), jnp.concatenate([hot, hot], axis=0), preferred_element_type=jnp.float32
    )
    place = place & (count - 1)
    total = jnp.zeros((COLS, PICKS), jnp.float32)
    for n in range(count):
        total = total + jnp.where(place == n, parts[n * COLS : (n + 1) * COLS, :], 0.0)
    sketch[...] = total
    first = pltpu.make_async_copy(sketch, sketch_hbm, sent.at[0])
    first.start()
    products = []
    for a in range(COLS):
        product = total * total[a : a + 1, :]
        products.append(sum(product[:, t * LANES : (t + 1) * LANES] for t in range(SLOTS)))
    products = jnp.concatenate(products + [jnp.zeros((LANES - COLS * COLS, LANES), jnp.float32)], axis=0)
    products = jnp.sum(products.T, axis=0, keepdims=True) * (1.0 / PICKS)
    gram[...] = products[:, : COLS * COLS]
    second = pltpu.make_async_copy(gram, gram_hbm, sent.at[1])
    second.start()
    first.wait()
    second.wait()


def on_device(matrix, flips, owners, offsets):
    f32, i32 = jnp.float32, jnp.int32
    params = pltpu.CompilerParams(vmem_limit_bytes=32 * 2**20)
    owners = owners.reshape(1, PICKS)
    offsets = offsets.reshape(1, PICKS)
    owners_other = other_core(owners)
    offsets_other = other_core(offsets)
    message_shape = jax.ShapeDtypeStruct((CHIPS * CHUNK, LANES), f32)
    picks_shape = jax.ShapeDtypeStruct((1, PICKS), i32)
    matrix, flips, own, slots = pl.pallas_call(
        load_kernel,
        name="load_and_requests",
        out_shape=(
            jax.ShapeDtypeStruct((COLS, LANES * LANES), f32),
            jax.ShapeDtypeStruct((LANES, LANES), i32),
            jax.ShapeDtypeStruct((HALVES * SLOTS, LANES), f32),
            picks_shape,
        ),
        in_specs=[HBM] * 4,
        out_specs=(VMEM, VMEM, VMEM, VMEM),
        scratch_shapes=[
            pltpu.VMEM((1, PICKS), i32),
            pltpu.VMEM((1, PICKS), i32),
            pltpu.SemaphoreType.DMA((3 + PIECES,)),
        ],
        compiler_params=params,
        cost_estimate=pl.CostEstimate(flops=2**22, bytes_accessed=4 * 2**20, transcendentals=0),
    )(
        *(
            pltpu.with_memory_space_constraint(operand, pltpu.HBM)
            for operand in (matrix, flips.reshape(LANES, LANES), owners, offsets)
        )
    )
    message = pl.pallas_call(
        send_kernel,
        name="transform_and_requests",
        out_shape=message_shape,
        in_specs=[VMEM] * 5,
        out_specs=VMEM,
        scratch_shapes=[pltpu.VMEM((LANES, COLS, LANES), f32)],
        compiler_params=params,
    )(matrix, flips, own, owners_other, offsets_other)
    message = exchange(message, FIRST)
    reply_shape = jax.ShapeDtypeStruct((CHIPS, LANES), f32)
    tables = [pltpu.VMEM((2 * LANES, PICKS), jnp.bfloat16), pltpu.VMEM((CHIPS, PICKS), f32)]
    theirs, left = pl.pallas_call(
        answer_other_kernel,
        name="answer_other",
        out_shape=(reply_shape, jax.ShapeDtypeStruct((HALVES, CHIPS * COLS, 2 * LANES), jnp.bfloat16)),
        in_specs=[VMEM],
        out_specs=(VMEM, VMEM),
        scratch_shapes=tables,
        compiler_params=params,
    )(message)
    theirs = other_core(theirs)
    mine = pl.pallas_call(
        answer_own_kernel,
        name="answer_own",
        out_shape=reply_shape,
        in_specs=[VMEM, VMEM],
        out_specs=VMEM,
        scratch_shapes=tables,
        compiler_params=params,
        cost_estimate=pl.CostEstimate(flops=2**28, bytes_accessed=2**21, transcendentals=0),
    )(message, left)
    reply = exchange(mine + theirs, FIRST_BACK)
    sketch, gram = pl.pallas_call(
        finish_kernel,
        name="finish",
        out_shape=(jax.ShapeDtypeStruct((COLS, PICKS), f32), jax.ShapeDtypeStruct((1, COLS * COLS), f32)),
        in_specs=[VMEM] * 2,
        out_specs=(HBM, HBM),
        scratch_shapes=[
            pltpu.VMEM((COLS, PICKS), f32),
            pltpu.VMEM((1, COLS * COLS), f32),
            pltpu.SemaphoreType.DMA((2,)),
        ],
        compiler_params=params,
    )(reply, slots)
    return sketch, gram.reshape(COLS * COLS, 1)


def solution(mesh):
    flat = Mesh(mesh.devices.reshape(-1), ("all",))
    in_specs = (P(None, "all"), P("all"), P("all", None), P("all"))
    out_specs = (P(None, "all"), P(None, "all"))
    return jax.shard_map(on_device, mesh=flat, in_specs=in_specs, out_specs=out_specs, check_vma=False)
```

```python
import math

import jax
import jax.numpy as jnp
from jax import lax
from jax.experimental import pallas as pl
from jax.experimental.pallas import tpu as pltpu
from jax.sharding import Mesh
from jax.sharding import PartitionSpec as P

LANES = 128
CHIPS = 64
HALVES = 2
SLOTS = 8
COLS = 8
CHUNK = HALVES * COLS + 1
PICKS = LANES * SLOTS
PIECES = 1
FIRST = 46
FIRST_BACK = 42
VMEM = pl.BlockSpec(memory_space=pltpu.VMEM)
HBM = pl.BlockSpec(memory_space=pltpu.HBM)


def device(chip, core):
    return (chip >> 2) * 8 + core * 4 + (chip & 3)


def exchange(rows, first):
    groups = [[device(j ^ first, core) for j in range(CHIPS)] for core in range(2)]
    parts = rows.reshape(CHIPS, 1, -1)
    parts = lax.all_to_all(parts, "all", split_axis=0, concat_axis=0, tiled=True, axis_index_groups=groups)
    return parts.reshape(rows.shape)


def other_core(value):
    return lax.ppermute(value, "all", [(i, i ^ 4) for i in range(2 * CHIPS)])


def walsh(tiles):
    span = 1
    while span < len(tiles):
        out = list(tiles)
        for i in range(len(tiles)):
            if not i & span:
                out[i] = tiles[i] + tiles[i | span]
                out[i | span] = tiles[i] - tiles[i | span]
        tiles = out
        span *= 2
    return tiles


def one_hot(index, count):
    rows = lax.broadcasted_iota(jnp.int32, (count, index.shape[1]), 0)
    return (rows == index).astype(jnp.float32)


def split(values):
    high = values.astype(jnp.bfloat16)
    return high, (values - high.astype(jnp.float32)).astype(jnp.bfloat16)


def requests(place, owner):
    section = lax.shift_right_logical(place, 7)
    part = lax.shift_right_logical(section, 1) ^ FIRST
    mask = lax.broadcasted_iota(jnp.int32, (LANES, PICKS), 0) == (section & 1) * CHIPS + part
    hot = jnp.where(mask, 1.0, 0.0)
    first = lax.broadcasted_iota(jnp.int32, (2 * LANES, LANES), 0)
    second = lax.broadcasted_iota(jnp.int32, (2 * LANES, LANES), 1)
    table = jnp.where((first < second) | (first >= LANES), 1.0, 0.0).astype(jnp.bfloat16)
    earlier = jnp.zeros((LANES, LANES), jnp.float32)
    ranks = []
    for t in range(SLOTS):
        cut = slice(t * LANES, (t + 1) * LANES)
        some = hot[:, cut]
        before = jnp.concatenate([some, earlier], axis=1).astype(jnp.bfloat16)
        count = jnp.dot(before, table, preferred_element_type=jnp.float32)
        ranks.append(jnp.sum(jnp.where(mask[:, cut], count, 0.0), axis=0, keepdims=True))
        earlier = earlier + some
    rank = jnp.concatenate(ranks, axis=1).astype(jnp.int32)
    slot = lax.broadcasted_iota(jnp.int32, (SLOTS, PICKS), 0) == rank
    low = (place & (LANES - 1)).astype(jnp.float32)
    wanted = jnp.concatenate(
        [jnp.where(slot, owner.astype(jnp.float32), 0.0), jnp.where(slot, low, 0.0)], axis=0
    )
    found = lax.dot_general(
        wanted.astype(jnp.bfloat16),
        hot.astype(jnp.bfloat16),
        (((1,), (1,)), ((), ())),
        preferred_element_type=jnp.float32,
    )
    column = lax.broadcasted_iota(jnp.int32, (SLOTS, LANES), 1)
    section_of = (((column & (CHIPS - 1)) ^ FIRST) * 2 + lax.shift_right_logical(column, 6)).astype(jnp.float32)
    rows = found[:SLOTS] * float(LANES * LANES) + section_of * float(LANES) + found[SLOTS:]
    return rank, jnp.concatenate([rows, pltpu.roll(rows, CHIPS, 1)], axis=0)


def load_kernel(
    matrix_hbm, flips_hbm, owners_hbm, offsets_hbm, matrix, flips, own, slots, owners, offsets, arrived
):
    copies = [
        pltpu.make_async_copy(source, target, arrived.at[i])
        for i, (source, target) in enumerate(
            ((flips_hbm, flips), (owners_hbm, owners), (offsets_hbm, offsets))
        )
    ]
    width = matrix.shape[1] // PIECES
    for p in range(PIECES):
        cut = pl.ds(p * width, width)
        copies.append(pltpu.make_async_copy(matrix_hbm.at[:, cut], matrix.at[:, cut], arrived.at[3 + p]))
    for copy in copies[2:0:-1] + copies[3:] + copies[:1]:
        copy.start()
    copies[1].wait()
    copies[2].wait()
    place = offsets[...]
    rank, rows = requests(place, owners[...])
    own[...] = rows
    section = lax.shift_right_logical(place, 7)
    part = lax.shift_right_logical(section, 1) ^ FIRST_BACK
    slot = (section & 1) * SLOTS + rank
    slots[...] = part * (HALVES * SLOTS) + (slot & 1) * SLOTS + lax.shift_right_logical(slot, 1)
    for copy in [copies[0]] + copies[3:]:
        copy.wait()


def send_kernel(matrix, flips, own, owners, offsets, message, mid):
    _, rows = requests(offsets[...], owners[...])
    rest = jnp.zeros((CHIPS, LANES - 2 * HALVES * SLOTS), jnp.float32)
    rows = jnp.concatenate([own[...], rows], axis=0).T[:CHIPS]
    message[pl.ds(CHUNK - 1, CHIPS, stride=CHUNK), :] = jnp.concatenate([rows, rest], axis=1)
    scale = 1.0 / math.sqrt(float(LANES) ** 3)
    signs = jnp.where(flips[...] == 1, scale, -scale)
    for i in range(16):
        tiles = []
        for f in range(i * 8, i * 8 + 8):
            tiles.append(matrix[:, f * LANES : (f + 1) * LANES] * signs[f : f + 1, :])
        for j, tile in enumerate(walsh(tiles)):
            mid[i * 8 + j] = tile
    for j in range(8):
        for i, tile in enumerate(walsh([mid[i * 8 + j] for i in range(16)])):
            section = i * 8 + j
            row = ((section >> 1) ^ FIRST) * CHUNK + (section & 1) * COLS
            message[pl.ds(row, COLS), :] = tile


def bit_sign(index, bit):
    return 1.0 - 2.0 * (lax.shift_right_logical(index, bit) & 1).astype(jnp.float32)


def sign_table(index, bits):
    row = lax.broadcasted_iota(jnp.int32, (8, index.shape[1]), 0)
    block = jnp.ones((8, index.shape[1]), jnp.float32)
    for b in range(3):
        block = block * jnp.where(lax.shift_right_logical(row, b) & 1 == 1, bit_sign(index, b), 1.0)
    blocks = [block]
    for b in range(3, bits):
        factor = bit_sign(index, b)
        blocks = blocks + [block * factor for block in blocks]
    return jnp.concatenate(blocks, axis=0)


def reorder(rows, flip):
    tiles = [rows[8 * i : 8 * i + 8] for i in range(rows.shape[0] // 8)]
    tiles = [tiles[i ^ (flip >> 3)] for i in range(len(tiles))]
    return jnp.concatenate([pltpu.roll(tile, 4, 0) if flip & 4 else tile for tile in tiles], axis=0)


def answer(message, kind, left, reply, right, signs):
    core = lax.shift_right_logical(lax.axis_index("all"), 2) & 1
    count = HALVES * SLOTS
    wanted = reorder(message[pl.ds(CHUNK - 1, CHIPS, stride=CHUNK), :], FIRST ^ FIRST_BACK)
    even, odd = [(LANES - kind * count - n) % LANES for n in range(2)]
    wanted = jnp.concatenate([pltpu.roll(wanted, even, 1) if even else wanted, pltpu.roll(wanted, odd, 1)], axis=0)
    wanted = wanted[:, :count].T.astype(jnp.int32)
    factors = []
    for n in range(count // 2):
        index = wanted[2 * n : 2 * n + 1, :]
        cut = slice(n * LANES, (n + 1) * LANES)
        table = sign_table(index & (LANES - 1), 7).astype(jnp.bfloat16)
        right[:LANES, cut] = table
        right[LANES:, cut] = table
        owner = lax.shift_right_logical(index, 14)
        chip = lax.shift_right_logical(owner, 3) * 4 + (owner & 3)
        signs[:, cut] = sign_table(chip, 6)
        factor = bit_sign(owner & (core * 4), 2)
        for b in range(6):
            if FIRST >> b & 1:
                factor = factor * bit_sign(chip, b)
        factors.append(factor)
    answers = []
    width = 256
    for half in range(HALVES):
        for n in range(PICKS // 2 // width):
            cut = slice(half * PICKS // 2 + n * width, half * PICKS // 2 + (n + 1) * width)
            total = jnp.zeros((COLS, width), jnp.float32)
            for m in range(2):
                part = jnp.dot(
                    left[half, m * 256 : (m + 1) * 256, :], right[:, cut], preferred_element_type=jnp.float32
                )
                for j in range(32):
                    total = total + part[j * COLS : (j + 1) * COLS, :] * signs[m * 32 + j : m * 32 + j + 1, cut]
            answers += [total[:, :LANES], total[:, LANES:]]
    answers = jnp.concatenate([answer * factor for answer, factor in zip(answers, factors)], axis=0)
    reply[...] = jnp.concatenate([answers, pltpu.roll(answers, CHIPS, 1)], axis=0).T[:CHIPS]


def answer_other_kernel(message, reply, left, right, signs):
    for half in range(HALVES):
        for pair in range(CHIPS // 2):
            tile = jnp.concatenate(
                [message[pl.ds(j * CHUNK + half * COLS, COLS), :] for j in (2 * pair, 2 * pair + 1)], axis=0
            )
            high, low = split(tile)
            left[half, pl.ds(pair * 16, 16), :LANES] = high
            left[half, pl.ds(pair * 16, 16), LANES:] = low
    answer(message, 1, left, reply, right, signs)


def answer_own_kernel(message, left, reply, right, signs):
    answer(message, 0, left, reply, right, signs)


def finish_kernel(reply, slots, sketch_hbm, gram_hbm, sketch, gram, sent):
    count = HALVES * SLOTS
    place = slots[...]
    hot = one_hot(lax.shift_right_logical(place, 4), CHIPS).astype(jnp.bfloat16)
    answers = jnp.concatenate([part.astype(jnp.float32) for part in split(reply[...])], axis=0)
    parts = jnp.dot(
        answers.T.astype(jnp.bfloat16), jnp.concatenate([hot, hot], axis=0), preferred_element_type=jnp.float32
    )
    place = place & (count - 1)
    total = jnp.zeros((COLS, PICKS), jnp.float32)
    for n in range(count):
        total = total + jnp.where(place == n, parts[n * COLS : (n + 1) * COLS, :], 0.0)
    sketch[...] = total
    first = pltpu.make_async_copy(sketch, sketch_hbm, sent.at[0])
    first.start()
    products = []
    for a in range(COLS):
        product = total * total[a : a + 1, :]
        products.append(sum(product[:, t * LANES : (t + 1) * LANES] for t in range(SLOTS)))
    products = jnp.concatenate(products + [jnp.zeros((LANES - COLS * COLS, LANES), jnp.float32)], axis=0)
    products = jnp.sum(products.T, axis=0, keepdims=True) * (1.0 / PICKS)
    gram[...] = products[:, : COLS * COLS]
    second = pltpu.make_async_copy(gram, gram_hbm, sent.at[1])
    second.start()
    first.wait()
    second.wait()


def on_device(matrix, flips, owners, offsets):
    f32, i32 = jnp.float32, jnp.int32
    params = pltpu.CompilerParams(vmem_limit_bytes=32 * 2**20)
    owners = owners.reshape(1, PICKS)
    offsets = offsets.reshape(1, PICKS)
    owners_other = other_core(owners)
    offsets_other = other_core(offsets)
    message_shape = jax.ShapeDtypeStruct((CHIPS * CHUNK, LANES), f32)
    picks_shape = jax.ShapeDtypeStruct((1, PICKS), i32)
    matrix, flips, own, slots = pl.pallas_call(
        load_kernel,
        name="load_and_requests",
        out_shape=(
            jax.ShapeDtypeStruct((COLS, LANES * LANES), f32),
            jax.ShapeDtypeStruct((LANES, LANES), i32),
            jax.ShapeDtypeStruct((HALVES * SLOTS, LANES), f32),
            picks_shape,
        ),
        in_specs=[HBM] * 4,
        out_specs=(VMEM, VMEM, VMEM, VMEM),
        scratch_shapes=[
            pltpu.VMEM((1, PICKS), i32),
            pltpu.VMEM((1, PICKS), i32),
            pltpu.SemaphoreType.DMA((3 + PIECES,)),
        ],
        compiler_params=params,
        cost_estimate=pl.CostEstimate(flops=2**22, bytes_accessed=4 * 2**20, transcendentals=0),
    )(
        *(
            pltpu.with_memory_space_constraint(operand, pltpu.HBM)
            for operand in (matrix, flips.reshape(LANES, LANES), owners, offsets)
        )
    )
    message = pl.pallas_call(
        send_kernel,
        name="transform_and_requests",
        out_shape=message_shape,
        in_specs=[VMEM] * 5,
        out_specs=VMEM,
        scratch_shapes=[pltpu.VMEM((LANES, COLS, LANES), f32)],
        compiler_params=params,
    )(matrix, flips, own, owners_other, offsets_other)
    message = exchange(message, FIRST)
    reply_shape = jax.ShapeDtypeStruct((CHIPS, LANES), f32)
    tables = [pltpu.VMEM((2 * LANES, PICKS), jnp.bfloat16), pltpu.VMEM((CHIPS, PICKS), f32)]
    theirs, left = pl.pallas_call(
        answer_other_kernel,
        name="answer_other",
        out_shape=(reply_shape, jax.ShapeDtypeStruct((HALVES, CHIPS * COLS, 2 * LANES), jnp.bfloat16)),
        in_specs=[VMEM],
        out_specs=(VMEM, VMEM),
        scratch_shapes=tables,
        compiler_params=params,
    )(message)
    theirs = other_core(theirs)
    mine = pl.pallas_call(
        answer_own_kernel,
        name="answer_own",
        out_shape=reply_shape,
        in_specs=[VMEM, VMEM],
        out_specs=VMEM,
        scratch_shapes=tables,
        compiler_params=params,
        cost_estimate=pl.CostEstimate(flops=2**28, bytes_accessed=2**21, transcendentals=0),
    )(message, left)
    reply = exchange(mine + theirs, FIRST_BACK)
    sketch, gram = pl.pallas_call(
        finish_kernel,
        name="finish",
        out_shape=(jax.ShapeDtypeStruct((COLS, PICKS), f32), jax.ShapeDtypeStruct((1, COLS * COLS), f32)),
        in_specs=[VMEM] * 2,
        out_specs=(HBM, HBM),
        scratch_shapes=[
            pltpu.VMEM((COLS, PICKS), f32),
            pltpu.VMEM((1, COLS * COLS), f32),
            pltpu.SemaphoreType.DMA((2,)),
        ],
        compiler_params=params,
    )(reply, slots)
    return sketch, gram.reshape(COLS * COLS, 1)


def solution(mesh):
    flat = Mesh(mesh.devices.reshape(-1), ("all",))
    in_specs = (P(None, "all"), P("all"), P("all", None), P("all"))
    out_specs = (P(None, "all"), P(None, "all"))
    return jax.shard_map(on_device, mesh=flat, in_specs=in_specs, out_specs=out_specs, check_vma=False)
```

```python
import math

import jax
import jax.numpy as jnp
from jax import lax
from jax.experimental import pallas as pl
from jax.experimental.pallas import tpu as pltpu
from jax.sharding import Mesh
from jax.sharding import PartitionSpec as P

LANES = 128
CHIPS = 64
HALVES = 2
SLOTS = 8
COLS = 8
CHUNK = HALVES * COLS + 1
PICKS = LANES * SLOTS
PIECES = 1
FIRST = 46
FIRST_BACK = 42
VMEM = pl.BlockSpec(memory_space=pltpu.VMEM)
HBM = pl.BlockSpec(memory_space=pltpu.HBM)


def device(chip, core):
    return (chip >> 2) * 8 + core * 4 + (chip & 3)


def exchange(rows, first):
    groups = [[device(j ^ first, core) for j in range(CHIPS)] for core in range(2)]
    parts = rows.reshape(CHIPS, 1, -1)
    parts = lax.all_to_all(parts, "all", split_axis=0, concat_axis=0, tiled=True, axis_index_groups=groups)
    return parts.reshape(rows.shape)


def other_core(value):
    return lax.ppermute(value, "all", [(i, i ^ 4) for i in range(2 * CHIPS)])


def walsh(tiles):
    span = 1
    while span < len(tiles):
        out = list(tiles)
        for i in range(len(tiles)):
            if not i & span:
                out[i] = tiles[i] + tiles[i | span]
                out[i | span] = tiles[i] - tiles[i | span]
        tiles = out
        span *= 2
    return tiles


def one_hot(index, count):
    rows = lax.broadcasted_iota(jnp.int32, (count, index.shape[1]), 0)
    return (rows == index).astype(jnp.float32)


def split(values):
    high = values.astype(jnp.bfloat16)
    return high, (values - high.astype(jnp.float32)).astype(jnp.bfloat16)


def requests(place, owner):
    section = lax.shift_right_logical(place, 7)
    part = lax.shift_right_logical(section, 1) ^ FIRST
    mask = lax.broadcasted_iota(jnp.int32, (LANES, PICKS), 0) == (section & 1) * CHIPS + part
    hot = jnp.where(mask, 1.0, 0.0)
    first = lax.broadcasted_iota(jnp.int32, (2 * LANES, LANES), 0)
    second = lax.broadcasted_iota(jnp.int32, (2 * LANES, LANES), 1)
    table = jnp.where((first < second) | (first >= LANES), 1.0, 0.0).astype(jnp.bfloat16)
    earlier = jnp.zeros((LANES, LANES), jnp.float32)
    ranks = []
    for t in range(SLOTS):
        cut = slice(t * LANES, (t + 1) * LANES)
        some = hot[:, cut]
        before = jnp.concatenate([some, earlier], axis=1).astype(jnp.bfloat16)
        count = jnp.dot(before, table, preferred_element_type=jnp.float32)
        ranks.append(jnp.sum(jnp.where(mask[:, cut], count, 0.0), axis=0, keepdims=True))
        earlier = earlier + some
    rank = jnp.concatenate(ranks, axis=1).astype(jnp.int32)
    slot = lax.broadcasted_iota(jnp.int32, (SLOTS, PICKS), 0) == rank
    low = (place & (LANES - 1)).astype(jnp.float32)
    wanted = jnp.concatenate(
        [jnp.where(slot, owner.astype(jnp.float32), 0.0), jnp.where(slot, low, 0.0)], axis=0
    )
    found = lax.dot_general(
        wanted.astype(jnp.bfloat16),
        hot.astype(jnp.bfloat16),
        (((1,), (1,)), ((), ())),
        preferred_element_type=jnp.float32,
    )
    column = lax.broadcasted_iota(jnp.int32, (SLOTS, LANES), 1)
    section_of = (((column & (CHIPS - 1)) ^ FIRST) * 2 + lax.shift_right_logical(column, 6)).astype(jnp.float32)
    rows = found[:SLOTS] * float(LANES * LANES) + section_of * float(LANES) + found[SLOTS:]
    return rank, jnp.concatenate([rows, pltpu.roll(rows, CHIPS, 1)], axis=0)


def load_kernel(
    matrix_hbm, flips_hbm, owners_hbm, offsets_hbm, matrix, flips, own, slots, owners, offsets, arrived
):
    copies = [
        pltpu.make_async_copy(source, target, arrived.at[i])
        for i, (source, target) in enumerate(
            ((flips_hbm, flips), (owners_hbm, owners), (offsets_hbm, offsets))
        )
    ]
    width = matrix.shape[1] // PIECES
    for p in range(PIECES):
        cut = pl.ds(p * width, width)
        copies.append(pltpu.make_async_copy(matrix_hbm.at[:, cut], matrix.at[:, cut], arrived.at[3 + p]))
    for copy in copies[2:0:-1] + copies[3:] + copies[:1]:
        copy.start()
    copies[1].wait()
    copies[2].wait()
    place = offsets[...]
    rank, rows = requests(place, owners[...])
    own[...] = rows
    section = lax.shift_right_logical(place, 7)
    part = lax.shift_right_logical(section, 1) ^ FIRST_BACK
    slot = (section & 1) * SLOTS + rank
    slots[...] = part * (HALVES * SLOTS) + (slot & 1) * SLOTS + lax.shift_right_logical(slot, 1)
    for copy in [copies[0]] + copies[3:]:
        copy.wait()


def send_kernel(matrix, flips, own, owners, offsets, message, mid):
    _, rows = requests(offsets[...], owners[...])
    rest = jnp.zeros((CHIPS, LANES - 2 * HALVES * SLOTS), jnp.float32)
    rows = jnp.concatenate([own[...], rows], axis=0).T[:CHIPS]
    message[pl.ds(CHUNK - 1, CHIPS, stride=CHUNK), :] = jnp.concatenate([rows, rest], axis=1)
    scale = 1.0 / math.sqrt(float(LANES) ** 3)
    signs = jnp.where(flips[...] == 1, scale, -scale)
    for i in range(16):
        tiles = []
        for f in range(i * 8, i * 8 + 8):
            tiles.append(matrix[:, f * LANES : (f + 1) * LANES] * signs[f : f + 1, :])
        for j, tile in enumerate(walsh(tiles)):
            mid[i * 8 + j] = tile
    for j in range(8):
        for i, tile in enumerate(walsh([mid[i * 8 + j] for i in range(16)])):
            section = i * 8 + j
            row = ((section >> 1) ^ FIRST) * CHUNK + (section & 1) * COLS
            message[pl.ds(row, COLS), :] = tile


def bit_sign(index, bit):
    return 1.0 - 2.0 * (lax.shift_right_logical(index, bit) & 1).astype(jnp.float32)


def sign_table(index, bits):
    row = lax.broadcasted_iota(jnp.int32, (8, index.shape[1]), 0)
    block = jnp.ones((8, index.shape[1]), jnp.float32)
    for b in range(3):
        block = block * jnp.where(lax.shift_right_logical(row, b) & 1 == 1, bit_sign(index, b), 1.0)
    blocks = [block]
    for b in range(3, bits):
        factor = bit_sign(index, b)
        blocks = blocks + [block * factor for block in blocks]
    return jnp.concatenate(blocks, axis=0)


def reorder(rows, flip):
    tiles = [rows[8 * i : 8 * i + 8] for i in range(rows.shape[0] // 8)]
    tiles = [tiles[i ^ (flip >> 3)] for i in range(len(tiles))]
    return jnp.concatenate([pltpu.roll(tile, 4, 0) if flip & 4 else tile for tile in tiles], axis=0)


def answer(message, kind, left, reply, right):
    core = lax.shift_right_logical(lax.axis_index("all"), 2) & 1
    count = HALVES * SLOTS
    wanted = reorder(message[pl.ds(CHUNK - 1, CHIPS, stride=CHUNK), :], FIRST ^ FIRST_BACK)
    even, odd = [(LANES - kind * count - n) % LANES for n in range(2)]
    wanted = jnp.concatenate([pltpu.roll(wanted, even, 1) if even else wanted, pltpu.roll(wanted, odd, 1)], axis=0)
    wanted = wanted[:, :count].T.astype(jnp.int32)
    factors, spread = [], []
    for n in range(count // 2):
        index = wanted[2 * n : 2 * n + 1, :]
        cut = slice(n * LANES, (n + 1) * LANES)
        table = sign_table(index & (LANES - 1), 7).astype(jnp.bfloat16)
        right[:LANES, cut] = table
        right[LANES:, cut] = table
        owner = lax.shift_right_logical(index, 14)
        chip = lax.shift_right_logical(owner, 3) * 4 + (owner & 3)
        bits = [bit_sign(chip, b) for b in range(6)]
        spread.append([jnp.broadcast_to(bit, (COLS, LANES)) for bit in bits])
        factor = bit_sign(owner & (core * 4), 2)
        for b in range(6):
            if FIRST >> b & 1:
                factor = factor * bits[b]
        factors.append(factor)
    answers = []
    width = 256
    for half in range(HALVES):
        for n in range(PICKS // 2 // width):
            cut = slice(half * PICKS // 2 + n * width, half * PICKS // 2 + (n + 1) * width)
            stacks = [[] for _ in range(width // LANES)]
            for m in range(4):
                part = jnp.dot(
                    left[half, m * 128 : (m + 1) * 128, :], right[:, cut], preferred_element_type=jnp.float32
                )
                for j in range(16):
                    for i, stack in enumerate(stacks):
                        tile = part[j * COLS : (j + 1) * COLS, i * LANES : (i + 1) * LANES]
                        signs = spread[(half * 2 + n) * 2 + i]
                        b = 0
                        while (m * 16 + j) >> b & 1:
                            tile = stack.pop() + tile * signs[b]
                            b += 1
                        stack.append(tile)
            answers += [stack[0] for stack in stacks]
    answers = jnp.concatenate([answer * factor for answer, factor in zip(answers, factors)], axis=0)
    reply[...] = jnp.concatenate([answers, pltpu.roll(answers, CHIPS, 1)], axis=0).T[:CHIPS]


def answer_other_kernel(message, reply, left, right):
    for half in range(HALVES):
        for pair in range(CHIPS // 2):
            tile = jnp.concatenate(
                [message[pl.ds(j * CHUNK + half * COLS, COLS), :] for j in (2 * pair, 2 * pair + 1)], axis=0
            )
            high, low = split(tile)
            left[half, pl.ds(pair * 16, 16), :LANES] = high
            left[half, pl.ds(pair * 16, 16), LANES:] = low
    answer(message, 1, left, reply, right)


def answer_own_kernel(message, left, reply, right):
    answer(message, 0, left, reply, right)


def finish_kernel(reply, slots, sketch_hbm, gram_hbm, sketch, gram, sent):
    count = HALVES * SLOTS
    place = slots[...]
    hot = one_hot(lax.shift_right_logical(place, 4), CHIPS).astype(jnp.bfloat16)
    answers = jnp.concatenate([part.astype(jnp.float32) for part in split(reply[...])], axis=0)
    parts = jnp.dot(
        answers.T.astype(jnp.bfloat16), jnp.concatenate([hot, hot], axis=0), preferred_element_type=jnp.float32
    )
    place = place & (count - 1)
    total = jnp.zeros((COLS, PICKS), jnp.float32)
    for n in range(count):
        total = total + jnp.where(place == n, parts[n * COLS : (n + 1) * COLS, :], 0.0)
    sketch[...] = total
    first = pltpu.make_async_copy(sketch, sketch_hbm, sent.at[0])
    first.start()
    products = []
    for a in range(COLS):
        product = total * total[a : a + 1, :]
        products.append(sum(product[:, t * LANES : (t + 1) * LANES] for t in range(SLOTS)))
    products = jnp.concatenate(products + [jnp.zeros((LANES - COLS * COLS, LANES), jnp.float32)], axis=0)
    products = jnp.sum(products.T, axis=0, keepdims=True) * (1.0 / PICKS)
    gram[...] = products[:, : COLS * COLS]
    second = pltpu.make_async_copy(gram, gram_hbm, sent.at[1])
    second.start()
    first.wait()
    second.wait()


def on_device(matrix, flips, owners, offsets):
    f32, i32 = jnp.float32, jnp.int32
    params = pltpu.CompilerParams(vmem_limit_bytes=32 * 2**20)
    owners = owners.reshape(1, PICKS)
    offsets = offsets.reshape(1, PICKS)
    owners_other = other_core(owners)
    offsets_other = other_core(offsets)
    message_shape = jax.ShapeDtypeStruct((CHIPS * CHUNK, LANES), f32)
    picks_shape = jax.ShapeDtypeStruct((1, PICKS), i32)
    matrix, flips, own, slots = pl.pallas_call(
        load_kernel,
        name="load_and_requests",
        out_shape=(
            jax.ShapeDtypeStruct((COLS, LANES * LANES), f32),
            jax.ShapeDtypeStruct((LANES, LANES), i32),
            jax.ShapeDtypeStruct((HALVES * SLOTS, LANES), f32),
            picks_shape,
        ),
        in_specs=[HBM] * 4,
        out_specs=(VMEM, VMEM, VMEM, VMEM),
        scratch_shapes=[
            pltpu.VMEM((1, PICKS), i32),
            pltpu.VMEM((1, PICKS), i32),
            pltpu.SemaphoreType.DMA((3 + PIECES,)),
        ],
        compiler_params=params,
        cost_estimate=pl.CostEstimate(flops=2**22, bytes_accessed=4 * 2**20, transcendentals=0),
    )(
        *(
            pltpu.with_memory_space_constraint(operand, pltpu.HBM)
            for operand in (matrix, flips.reshape(LANES, LANES), owners, offsets)
        )
    )
    message = pl.pallas_call(
        send_kernel,
        name="transform_and_requests",
        out_shape=message_shape,
        in_specs=[VMEM] * 5,
        out_specs=VMEM,
        scratch_shapes=[pltpu.VMEM((LANES, COLS, LANES), f32)],
        compiler_params=params,
    )(matrix, flips, own, owners_other, offsets_other)
    message = exchange(message, FIRST)
    reply_shape = jax.ShapeDtypeStruct((CHIPS, LANES), f32)
    tables = [pltpu.VMEM((2 * LANES, PICKS), jnp.bfloat16)]
    theirs, left = pl.pallas_call(
        answer_other_kernel,
        name="answer_other",
        out_shape=(reply_shape, jax.ShapeDtypeStruct((HALVES, CHIPS * COLS, 2 * LANES), jnp.bfloat16)),
        in_specs=[VMEM],
        out_specs=(VMEM, VMEM),
        scratch_shapes=tables,
        compiler_params=params,
    )(message)
    theirs = other_core(theirs)
    mine = pl.pallas_call(
        answer_own_kernel,
        name="answer_own",
        out_shape=reply_shape,
        in_specs=[VMEM, VMEM],
        out_specs=VMEM,
        scratch_shapes=tables,
        compiler_params=params,
        cost_estimate=pl.CostEstimate(flops=2**28, bytes_accessed=2**21, transcendentals=0),
    )(message, left)
    reply = exchange(mine + theirs, FIRST_BACK)
    sketch, gram = pl.pallas_call(
        finish_kernel,
        name="finish",
        out_shape=(jax.ShapeDtypeStruct((COLS, PICKS), f32), jax.ShapeDtypeStruct((1, COLS * COLS), f32)),
        in_specs=[VMEM] * 2,
        out_specs=(HBM, HBM),
        scratch_shapes=[
            pltpu.VMEM((COLS, PICKS), f32),
            pltpu.VMEM((1, COLS * COLS), f32),
            pltpu.SemaphoreType.DMA((2,)),
        ],
        compiler_params=params,
    )(reply, slots)
    return sketch, gram.reshape(COLS * COLS, 1)


def solution(mesh):
    flat = Mesh(mesh.devices.reshape(-1), ("all",))
    in_specs = (P(None, "all"), P("all"), P("all", None), P("all"))
    out_specs = (P(None, "all"), P(None, "all"))
    return jax.shard_map(on_device, mesh=flat, in_specs=in_specs, out_specs=out_specs, check_vma=False)
```

```python
import math

import jax
import jax.numpy as jnp
from jax import lax
from jax.experimental import pallas as pl
from jax.experimental.pallas import tpu as pltpu
from jax.sharding import Mesh
from jax.sharding import PartitionSpec as P

LANES = 128
CHIPS = 64
HALVES = 2
SLOTS = 8
COLS = 8
CHUNK = HALVES * COLS + 1
PICKS = LANES * SLOTS
PIECES = 4
FIRST = 46
FIRST_BACK = 42
VMEM = pl.BlockSpec(memory_space=pltpu.VMEM)
HBM = pl.BlockSpec(memory_space=pltpu.HBM)


def device(chip, core):
    return (chip >> 2) * 8 + core * 4 + (chip & 3)


def exchange(rows, first):
    groups = [[device(j ^ first, core) for j in range(CHIPS)] for core in range(2)]
    parts = rows.reshape(CHIPS, 1, -1)
    parts = lax.all_to_all(parts, "all", split_axis=0, concat_axis=0, tiled=True, axis_index_groups=groups)
    return parts.reshape(rows.shape)


def other_core(value):
    return lax.ppermute(value, "all", [(i, i ^ 4) for i in range(2 * CHIPS)])


def walsh(tiles):
    span = 1
    while span < len(tiles):
        out = list(tiles)
        for i in range(len(tiles)):
            if not i & span:
                out[i] = tiles[i] + tiles[i | span]
                out[i | span] = tiles[i] - tiles[i | span]
        tiles = out
        span *= 2
    return tiles


def one_hot(index, count):
    rows = lax.broadcasted_iota(jnp.int32, (count, index.shape[1]), 0)
    return (rows == index).astype(jnp.float32)


def split(values):
    high = values.astype(jnp.bfloat16)
    return high, (values - high.astype(jnp.float32)).astype(jnp.bfloat16)


def requests(place, owner):
    section = lax.shift_right_logical(place, 7)
    part = lax.shift_right_logical(section, 1) ^ FIRST
    mask = lax.broadcasted_iota(jnp.int32, (LANES, PICKS), 0) == (section & 1) * CHIPS + part
    hot = jnp.where(mask, 1.0, 0.0)
    first = lax.broadcasted_iota(jnp.int32, (2 * LANES, LANES), 0)
    second = lax.broadcasted_iota(jnp.int32, (2 * LANES, LANES), 1)
    table = jnp.where((first < second) | (first >= LANES), 1.0, 0.0).astype(jnp.bfloat16)
    earlier = jnp.zeros((LANES, LANES), jnp.float32)
    ranks = []
    for t in range(SLOTS):
        cut = slice(t * LANES, (t + 1) * LANES)
        some = hot[:, cut]
        before = jnp.concatenate([some, earlier], axis=1).astype(jnp.bfloat16)
        count = jnp.dot(before, table, preferred_element_type=jnp.float32)
        ranks.append(jnp.sum(jnp.where(mask[:, cut], count, 0.0), axis=0, keepdims=True))
        earlier = earlier + some
    rank = jnp.concatenate(ranks, axis=1).astype(jnp.int32)
    slot = lax.broadcasted_iota(jnp.int32, (SLOTS, PICKS), 0) == rank
    low = (place & (LANES - 1)).astype(jnp.float32)
    wanted = jnp.concatenate(
        [jnp.where(slot, owner.astype(jnp.float32), 0.0), jnp.where(slot, low, 0.0)], axis=0
    )
    found = lax.dot_general(
        wanted.astype(jnp.bfloat16),
        hot.astype(jnp.bfloat16),
        (((1,), (1,)), ((), ())),
        preferred_element_type=jnp.float32,
    )
    column = lax.broadcasted_iota(jnp.int32, (SLOTS, LANES), 1)
    section_of = (((column & (CHIPS - 1)) ^ FIRST) * 2 + lax.shift_right_logical(column, 6)).astype(jnp.float32)
    rows = found[:SLOTS] * float(LANES * LANES) + section_of * float(LANES) + found[SLOTS:]
    return rank, jnp.concatenate([rows, pltpu.roll(rows, CHIPS, 1)], axis=0)


def load_kernel(
    matrix_hbm, flips_hbm, owners_hbm, offsets_hbm, matrix, flips, own, slots, owners, offsets, arrived
):
    copies = [
        pltpu.make_async_copy(source, target, arrived.at[i])
        for i, (source, target) in enumerate(
            ((flips_hbm, flips), (owners_hbm, owners), (offsets_hbm, offsets))
        )
    ]
    width = matrix.shape[1] // PIECES
    for p in range(PIECES):
        cut = pl.ds(p * width, width)
        copies.append(pltpu.make_async_copy(matrix_hbm.at[:, cut], matrix.at[:, cut], arrived.at[3 + p]))
    for copy in copies:
        copy.start()
    copies[1].wait()
    copies[2].wait()
    place = offsets[...]
    rank, rows = requests(place, owners[...])
    own[...] = rows
    section = lax.shift_right_logical(place, 7)
    part = lax.shift_right_logical(section, 1) ^ FIRST_BACK
    slot = (section & 1) * SLOTS + rank
    slots[...] = part * (HALVES * SLOTS) + (slot & 1) * SLOTS + lax.shift_right_logical(slot, 1)
    for copy in [copies[0]] + copies[3:]:
        copy.wait()


def send_kernel(matrix, flips, own, owners, offsets, message, mid):
    _, rows = requests(offsets[...], owners[...])
    rest = jnp.zeros((LANES - 2 * HALVES * SLOTS, LANES), jnp.float32)
    rows = jnp.concatenate([own[...], rows, rest], axis=0).T
    message[pl.ds(CHUNK - 1, CHIPS, stride=CHUNK), :] = rows[:CHIPS]
    scale = 1.0 / math.sqrt(float(LANES) ** 3)
    signs = jnp.where(flips[...] == 1, scale, -scale)
    for i in range(16):
        tiles = []
        for f in range(i * 8, i * 8 + 8):
            tiles.append(matrix[:, f * LANES : (f + 1) * LANES] * signs[f : f + 1, :])
        for j, tile in enumerate(walsh(tiles)):
            mid[i * 8 + j] = tile
    for j in range(8):
        for i, tile in enumerate(walsh([mid[i * 8 + j] for i in range(16)])):
            section = i * 8 + j
            row = ((section >> 1) ^ FIRST) * CHUNK + (section & 1) * COLS
            message[pl.ds(row, COLS), :] = tile


def bit_sign(index, bit):
    return 1.0 - 2.0 * (lax.shift_right_logical(index, bit) & 1).astype(jnp.float32)


def sign_table(index, bits):
    row = lax.broadcasted_iota(jnp.int32, (8, index.shape[1]), 0)
    block = jnp.ones((8, index.shape[1]), jnp.float32)
    for b in range(3):
        block = block * jnp.where(lax.shift_right_logical(row, b) & 1 == 1, bit_sign(index, b), 1.0)
    blocks = [block]
    for b in range(3, bits):
        factor = bit_sign(index, b)
        blocks = blocks + [block * factor for block in blocks]
    return jnp.concatenate(blocks, axis=0)


def reorder(rows, flip):
    tiles = [rows[8 * i : 8 * i + 8] for i in range(rows.shape[0] // 8)]
    tiles = [tiles[i ^ (flip >> 3)] for i in range(len(tiles))]
    return jnp.concatenate([pltpu.roll(tile, 4, 0) if flip & 4 else tile for tile in tiles], axis=0)


def answer(message, kind, left, reply, right):
    core = lax.shift_right_logical(lax.axis_index("all"), 2) & 1
    count = HALVES * SLOTS
    wanted = reorder(message[pl.ds(CHUNK - 1, CHIPS, stride=CHUNK), :], FIRST ^ FIRST_BACK)
    even, odd = [(LANES - kind * count - n) % LANES for n in range(2)]
    wanted = jnp.concatenate([pltpu.roll(wanted, even, 1) if even else wanted, pltpu.roll(wanted, odd, 1)], axis=0)
    wanted = wanted[:, :count].T.astype(jnp.int32)
    factors, spread = [], []
    for n in range(count // 2):
        index = wanted[2 * n : 2 * n + 1, :]
        cut = slice(n * LANES, (n + 1) * LANES)
        table = sign_table(index & (LANES - 1), 7).astype(jnp.bfloat16)
        right[:LANES, cut] = table
        right[LANES:, cut] = table
        owner = lax.shift_right_logical(index, 14)
        chip = lax.shift_right_logical(owner, 3) * 4 + (owner & 3)
        bits = [bit_sign(chip, b) for b in range(6)]
        spread.append([jnp.broadcast_to(bit, (COLS, LANES)) for bit in bits])
        factor = bit_sign(owner & (core * 4), 2)
        for b in range(6):
            if FIRST >> b & 1:
                factor = factor * bits[b]
        factors.append(factor)
    answers = []
    width = 256
    for half in range(HALVES):
        for n in range(PICKS // 2 // width):
            cut = slice(half * PICKS // 2 + n * width, half * PICKS // 2 + (n + 1) * width)
            stacks = [[] for _ in range(width // LANES)]
            for m in range(4):
                part = jnp.dot(
                    left[half, m * 128 : (m + 1) * 128, :], right[:, cut], preferred_element_type=jnp.float32
                )
                for j in range(16):
                    for i, stack in enumerate(stacks):
                        tile = part[j * COLS : (j + 1) * COLS, i * LANES : (i + 1) * LANES]
                        signs = spread[(half * 2 + n) * 2 + i]
                        b = 0
                        while (m * 16 + j) >> b & 1:
                            tile = stack.pop() + tile * signs[b]
                            b += 1
                        stack.append(tile)
            answers += [stack[0] for stack in stacks]
    answers = jnp.concatenate([answer * factor for answer, factor in zip(answers, factors)], axis=0)
    reply[...] = jnp.concatenate([answers, pltpu.roll(answers, CHIPS, 1)], axis=0).T[:CHIPS]


def answer_other_kernel(message, reply, left, right):
    for half in range(HALVES):
        for pair in range(CHIPS // 2):
            tile = jnp.concatenate(
                [message[pl.ds(j * CHUNK + half * COLS, COLS), :] for j in (2 * pair, 2 * pair + 1)], axis=0
            )
            high, low = split(tile)
            left[half, pl.ds(pair * 16, 16), :LANES] = high
            left[half, pl.ds(pair * 16, 16), LANES:] = low
    answer(message, 1, left, reply, right)


def answer_own_kernel(message, left, reply, right):
    answer(message, 0, left, reply, right)


def finish_kernel(reply, slots, sketch_hbm, gram_hbm, sketch, gram, sent):
    count = HALVES * SLOTS
    place = slots[...]
    hot = one_hot(lax.shift_right_logical(place, 4), CHIPS).astype(jnp.bfloat16)
    answers = jnp.concatenate([part.astype(jnp.float32) for part in split(reply[...])], axis=0)
    parts = jnp.dot(
        answers.T.astype(jnp.bfloat16), jnp.concatenate([hot, hot], axis=0), preferred_element_type=jnp.float32
    )
    place = place & (count - 1)
    total = jnp.zeros((COLS, PICKS), jnp.float32)
    for n in range(count):
        total = total + jnp.where(place == n, parts[n * COLS : (n + 1) * COLS, :], 0.0)
    sketch[...] = total
    first = pltpu.make_async_copy(sketch, sketch_hbm, sent.at[0])
    first.start()
    products = []
    for a in range(COLS):
        product = total * total[a : a + 1, :]
        products.append(sum(product[:, t * LANES : (t + 1) * LANES] for t in range(SLOTS)))
    products = jnp.concatenate(products + [jnp.zeros((LANES - COLS * COLS, LANES), jnp.float32)], axis=0)
    products = jnp.sum(products.T, axis=0, keepdims=True) * (1.0 / PICKS)
    gram[...] = products[:, : COLS * COLS]
    second = pltpu.make_async_copy(gram, gram_hbm, sent.at[1])
    second.start()
    first.wait()
    second.wait()


def on_device(matrix, flips, owners, offsets):
    f32, i32 = jnp.float32, jnp.int32
    params = pltpu.CompilerParams(vmem_limit_bytes=32 * 2**20)
    owners = owners.reshape(1, PICKS)
    offsets = offsets.reshape(1, PICKS)
    owners_other = other_core(owners)
    offsets_other = other_core(offsets)
    message_shape = jax.ShapeDtypeStruct((CHIPS * CHUNK, LANES), f32)
    picks_shape = jax.ShapeDtypeStruct((1, PICKS), i32)
    matrix, flips, own, slots = pl.pallas_call(
        load_kernel,
        name="load_and_requests",
        out_shape=(
            jax.ShapeDtypeStruct((COLS, LANES * LANES), f32),
            jax.ShapeDtypeStruct((LANES, LANES), i32),
            jax.ShapeDtypeStruct((HALVES * SLOTS, LANES), f32),
            picks_shape,
        ),
        in_specs=[HBM] * 4,
        out_specs=(VMEM, VMEM, VMEM, VMEM),
        scratch_shapes=[
            pltpu.VMEM((1, PICKS), i32),
            pltpu.VMEM((1, PICKS), i32),
            pltpu.SemaphoreType.DMA((3 + PIECES,)),
        ],
        compiler_params=params,
        cost_estimate=pl.CostEstimate(flops=2**22, bytes_accessed=4 * 2**20, transcendentals=0),
    )(
        *(
            pltpu.with_memory_space_constraint(operand, pltpu.HBM)
            for operand in (matrix, flips.reshape(LANES, LANES), owners, offsets)
        )
    )
    message = pl.pallas_call(
        send_kernel,
        name="transform_and_requests",
        out_shape=message_shape,
        in_specs=[VMEM] * 5,
        out_specs=VMEM,
        scratch_shapes=[pltpu.VMEM((LANES, COLS, LANES), f32)],
        compiler_params=params,
    )(matrix, flips, own, owners_other, offsets_other)
    message = exchange(message, FIRST)
    reply_shape = jax.ShapeDtypeStruct((CHIPS, LANES), f32)
    tables = [pltpu.VMEM((2 * LANES, PICKS), jnp.bfloat16)]
    theirs, left = pl.pallas_call(
        answer_other_kernel,
        name="answer_other",
        out_shape=(reply_shape, jax.ShapeDtypeStruct((HALVES, CHIPS * COLS, 2 * LANES), jnp.bfloat16)),
        in_specs=[VMEM],
        out_specs=(VMEM, VMEM),
        scratch_shapes=tables,
        compiler_params=params,
    )(message)
    theirs = other_core(theirs)
    mine = pl.pallas_call(
        answer_own_kernel,
        name="answer_own",
        out_shape=reply_shape,
        in_specs=[VMEM, VMEM],
        out_specs=VMEM,
        scratch_shapes=tables,
        compiler_params=params,
        cost_estimate=pl.CostEstimate(flops=2**28, bytes_accessed=2**21, transcendentals=0),
    )(message, left)
    reply = exchange(mine + theirs, FIRST_BACK)
    sketch, gram = pl.pallas_call(
        finish_kernel,
        name="finish",
        out_shape=(jax.ShapeDtypeStruct((COLS, PICKS), f32), jax.ShapeDtypeStruct((1, COLS * COLS), f32)),
        in_specs=[VMEM] * 2,
        out_specs=(HBM, HBM),
        scratch_shapes=[
            pltpu.VMEM((COLS, PICKS), f32),
            pltpu.VMEM((1, COLS * COLS), f32),
            pltpu.SemaphoreType.DMA((2,)),
        ],
        compiler_params=params,
    )(reply, slots)
    return sketch, gram.reshape(COLS * COLS, 1)


def solution(mesh):
    flat = Mesh(mesh.devices.reshape(-1), ("all",))
    in_specs = (P(None, "all"), P("all"), P("all", None), P("all"))
    out_specs = (P(None, "all"), P(None, "all"))
    return jax.shard_map(on_device, mesh=flat, in_specs=in_specs, out_specs=out_specs, check_vma=False)
```

```python
import math

import jax
import jax.numpy as jnp
from jax import lax
from jax.experimental import pallas as pl
from jax.experimental.pallas import tpu as pltpu
from jax.sharding import Mesh
from jax.sharding import PartitionSpec as P

LANES = 128
CHIPS = 64
HALVES = 2
SLOTS = 8
COLS = 8
CHUNK = HALVES * COLS + 1
PICKS = LANES * SLOTS
PIECES = 2
FIRST = 46
FIRST_BACK = 42
VMEM = pl.BlockSpec(memory_space=pltpu.VMEM)
HBM = pl.BlockSpec(memory_space=pltpu.HBM)


def device(chip, core):
    return (chip >> 2) * 8 + core * 4 + (chip & 3)


def exchange(rows, first):
    groups = [[device(j ^ first, core) for j in range(CHIPS)] for core in range(2)]
    parts = rows.reshape(CHIPS, 1, -1)
    parts = lax.all_to_all(parts, "all", split_axis=0, concat_axis=0, tiled=True, axis_index_groups=groups)
    return parts.reshape(rows.shape)


def other_core(value):
    return lax.ppermute(value, "all", [(i, i ^ 4) for i in range(2 * CHIPS)])


def walsh(tiles):
    span = 1
    while span < len(tiles):
        out = list(tiles)
        for i in range(len(tiles)):
            if not i & span:
                out[i] = tiles[i] + tiles[i | span]
                out[i | span] = tiles[i] - tiles[i | span]
        tiles = out
        span *= 2
    return tiles


def one_hot(index, count):
    rows = lax.broadcasted_iota(jnp.int32, (count, index.shape[1]), 0)
    return (rows == index).astype(jnp.float32)


def split(values):
    high = values.astype(jnp.bfloat16)
    return high, (values - high.astype(jnp.float32)).astype(jnp.bfloat16)


def requests(place, owner):
    section = lax.shift_right_logical(place, 7)
    part = lax.shift_right_logical(section, 1) ^ FIRST
    mask = lax.broadcasted_iota(jnp.int32, (LANES, PICKS), 0) == (section & 1) * CHIPS + part
    hot = jnp.where(mask, 1.0, 0.0)
    first = lax.broadcasted_iota(jnp.int32, (2 * LANES, LANES), 0)
    second = lax.broadcasted_iota(jnp.int32, (2 * LANES, LANES), 1)
    table = jnp.where((first < second) | (first >= LANES), 1.0, 0.0).astype(jnp.bfloat16)
    earlier = jnp.zeros((LANES, LANES), jnp.float32)
    ranks = []
    for t in range(SLOTS):
        cut = slice(t * LANES, (t + 1) * LANES)
        some = hot[:, cut]
        before = jnp.concatenate([some, earlier], axis=1).astype(jnp.bfloat16)
        count = jnp.dot(before, table, preferred_element_type=jnp.float32)
        ranks.append(jnp.sum(jnp.where(mask[:, cut], count, 0.0), axis=0, keepdims=True))
        earlier = earlier + some
    rank = jnp.concatenate(ranks, axis=1).astype(jnp.int32)
    slot = lax.broadcasted_iota(jnp.int32, (SLOTS, PICKS), 0) == rank
    low = (place & (LANES - 1)).astype(jnp.float32)
    wanted = jnp.concatenate(
        [jnp.where(slot, owner.astype(jnp.float32), 0.0), jnp.where(slot, low, 0.0)], axis=0
    )
    found = lax.dot_general(
        wanted.astype(jnp.bfloat16),
        hot.astype(jnp.bfloat16),
        (((1,), (1,)), ((), ())),
        preferred_element_type=jnp.float32,
    )
    column = lax.broadcasted_iota(jnp.int32, (SLOTS, LANES), 1)
    section_of = (((column & (CHIPS - 1)) ^ FIRST) * 2 + lax.shift_right_logical(column, 6)).astype(jnp.float32)
    rows = found[:SLOTS] * float(LANES * LANES) + section_of * float(LANES) + found[SLOTS:]
    return rank, jnp.concatenate([rows, pltpu.roll(rows, CHIPS, 1)], axis=0)


def load_kernel(
    matrix_hbm, flips_hbm, owners_hbm, offsets_hbm, matrix, flips, own, slots, owners, offsets, arrived
):
    copies = [
        pltpu.make_async_copy(source, target, arrived.at[i])
        for i, (source, target) in enumerate(
            ((flips_hbm, flips), (owners_hbm, owners), (offsets_hbm, offsets))
        )
    ]
    width = matrix.shape[1] // PIECES
    for p in range(PIECES):
        cut = pl.ds(p * width, width)
        copies.append(pltpu.make_async_copy(matrix_hbm.at[:, cut], matrix.at[:, cut], arrived.at[3 + p]))
    for copy in copies:
        copy.start()
    copies[1].wait()
    copies[2].wait()
    place = offsets[...]
    rank, rows = requests(place, owners[...])
    own[...] = rows
    section = lax.shift_right_logical(place, 7)
    part = lax.shift_right_logical(section, 1) ^ FIRST_BACK
    slot = (section & 1) * SLOTS + rank
    slots[...] = part * (HALVES * SLOTS) + (slot & 1) * SLOTS + lax.shift_right_logical(slot, 1)
    for copy in [copies[0]] + copies[3:]:
        copy.wait()


def send_kernel(matrix, flips, own, owners, offsets, message, mid):
    _, rows = requests(offsets[...], owners[...])
    rest = jnp.zeros((LANES - 2 * HALVES * SLOTS, LANES), jnp.float32)
    rows = jnp.concatenate([own[...], rows, rest], axis=0).T
    message[pl.ds(CHUNK - 1, CHIPS, stride=CHUNK), :] = rows[:CHIPS]
    scale = 1.0 / math.sqrt(float(LANES) ** 3)
    signs = jnp.where(flips[...] == 1, scale, -scale)
    for i in range(16):
        tiles = []
        for f in range(i * 8, i * 8 + 8):
            tiles.append(matrix[:, f * LANES : (f + 1) * LANES] * signs[f : f + 1, :])
        for j, tile in enumerate(walsh(tiles)):
            mid[i * 8 + j] = tile
    for j in range(8):
        for i, tile in enumerate(walsh([mid[i * 8 + j] for i in range(16)])):
            section = i * 8 + j
            row = ((section >> 1) ^ FIRST) * CHUNK + (section & 1) * COLS
            message[pl.ds(row, COLS), :] = tile


def bit_sign(index, bit):
    return 1.0 - 2.0 * (lax.shift_right_logical(index, bit) & 1).astype(jnp.float32)


def sign_table(index, bits):
    row = lax.broadcasted_iota(jnp.int32, (8, index.shape[1]), 0)
    block = jnp.ones((8, index.shape[1]), jnp.float32)
    for b in range(3):
        block = block * jnp.where(lax.shift_right_logical(row, b) & 1 == 1, bit_sign(index, b), 1.0)
    blocks = [block]
    for b in range(3, bits):
        factor = bit_sign(index, b)
        blocks = blocks + [block * factor for block in blocks]
    return jnp.concatenate(blocks, axis=0)


def reorder(rows, flip):
    tiles = [rows[8 * i : 8 * i + 8] for i in range(rows.shape[0] // 8)]
    tiles = [tiles[i ^ (flip >> 3)] for i in range(len(tiles))]
    return jnp.concatenate([pltpu.roll(tile, 4, 0) if flip & 4 else tile for tile in tiles], axis=0)


def answer(message, kind, left, reply, right, signs):
    core = lax.shift_right_logical(lax.axis_index("all"), 2) & 1
    count = HALVES * SLOTS
    wanted = reorder(message[pl.ds(CHUNK - 1, CHIPS, stride=CHUNK), :], FIRST ^ FIRST_BACK)
    even, odd = [(LANES - kind * count - n) % LANES for n in range(2)]
    wanted = jnp.concatenate([pltpu.roll(wanted, even, 1) if even else wanted, pltpu.roll(wanted, odd, 1)], axis=0)
    wanted = wanted.T[:count, :].astype(jnp.int32)
    factors = []
    for n in range(count // 2):
        index = wanted[2 * n : 2 * n + 1, :]
        cut = slice(n * LANES, (n + 1) * LANES)
        table = sign_table(index & (LANES - 1), 7).astype(jnp.bfloat16)
        right[:LANES, cut] = table
        right[LANES:, cut] = table
        owner = lax.shift_right_logical(index, 14)
        chip = lax.shift_right_logical(owner, 3) * 4 + (owner & 3)
        signs[:, cut] = sign_table(chip, 6)
        factor = bit_sign(owner & (core * 4), 2)
        for b in range(6):
            if FIRST >> b & 1:
                factor = factor * bit_sign(chip, b)
        factors.append(factor)
    answers = []
    width = 256
    for half in range(HALVES):
        for n in range(PICKS // 2 // width):
            cut = slice(half * PICKS // 2 + n * width, half * PICKS // 2 + (n + 1) * width)
            total = jnp.zeros((COLS, width), jnp.float32)
            for m in range(2):
                part = jnp.dot(
                    left[half, m * 256 : (m + 1) * 256, :], right[:, cut], preferred_element_type=jnp.float32
                )
                for j in range(32):
                    total = total + part[j * COLS : (j + 1) * COLS, :] * signs[m * 32 + j : m * 32 + j + 1, cut]
            answers += [total[:, :LANES], total[:, LANES:]]
    answers = jnp.concatenate([answer * factor for answer, factor in zip(answers, factors)], axis=0)
    reply[...] = jnp.concatenate([answers, pltpu.roll(answers, CHIPS, 1)], axis=0).T[:CHIPS]


def answer_other_kernel(message, reply, left, right, signs):
    for half in range(HALVES):
        for pair in range(CHIPS // 2):
            tile = jnp.concatenate(
                [message[pl.ds(j * CHUNK + half * COLS, COLS), :] for j in (2 * pair, 2 * pair + 1)], axis=0
            )
            high, low = split(tile)
            left[half, pl.ds(pair * 16, 16), :LANES] = high
            left[half, pl.ds(pair * 16, 16), LANES:] = low
    answer(message, 1, left, reply, right, signs)


def answer_own_kernel(message, left, reply, right, signs):
    answer(message, 0, left, reply, right, signs)


def finish_kernel(reply, slots, sketch_hbm, gram_hbm, sketch, gram, sent):
    count = HALVES * SLOTS
    place = slots[...]
    hot = one_hot(lax.shift_right_logical(place, 4), CHIPS).astype(jnp.bfloat16)
    answers = jnp.concatenate([part.astype(jnp.float32) for part in split(reply[...])], axis=0)
    parts = jnp.dot(
        answers.T.astype(jnp.bfloat16), jnp.concatenate([hot, hot], axis=0), preferred_element_type=jnp.float32
    )
    place = place & (count - 1)
    total = jnp.zeros((COLS, PICKS), jnp.float32)
    for n in range(count):
        total = total + jnp.where(place == n, parts[n * COLS : (n + 1) * COLS, :], 0.0)
    sketch[...] = total
    first = pltpu.make_async_copy(sketch, sketch_hbm, sent.at[0])
    first.start()
    products = []
    for a in range(COLS):
        product = total * total[a : a + 1, :]
        products.append(sum(product[:, t * LANES : (t + 1) * LANES] for t in range(SLOTS)))
    products = jnp.concatenate(products + [jnp.zeros((LANES - COLS * COLS, LANES), jnp.float32)], axis=0)
    products = jnp.sum(products.T, axis=0, keepdims=True) * (1.0 / PICKS)
    gram[...] = products[:, : COLS * COLS]
    second = pltpu.make_async_copy(gram, gram_hbm, sent.at[1])
    second.start()
    first.wait()
    second.wait()


def on_device(matrix, flips, owners, offsets):
    f32, i32 = jnp.float32, jnp.int32
    params = pltpu.CompilerParams(vmem_limit_bytes=32 * 2**20)
    owners = owners.reshape(1, PICKS)
    offsets = offsets.reshape(1, PICKS)
    owners_other = other_core(owners)
    offsets_other = other_core(offsets)
    message_shape = jax.ShapeDtypeStruct((CHIPS * CHUNK, LANES), f32)
    picks_shape = jax.ShapeDtypeStruct((1, PICKS), i32)
    matrix, flips, own, slots = pl.pallas_call(
        load_kernel,
        name="load_and_requests",
        out_shape=(
            jax.ShapeDtypeStruct((COLS, LANES * LANES), f32),
            jax.ShapeDtypeStruct((LANES, LANES), i32),
            jax.ShapeDtypeStruct((HALVES * SLOTS, LANES), f32),
            picks_shape,
        ),
        in_specs=[HBM] * 4,
        out_specs=(VMEM, VMEM, VMEM, VMEM),
        scratch_shapes=[
            pltpu.VMEM((1, PICKS), i32),
            pltpu.VMEM((1, PICKS), i32),
            pltpu.SemaphoreType.DMA((3 + PIECES,)),
        ],
        compiler_params=params,
        cost_estimate=pl.CostEstimate(flops=2**22, bytes_accessed=4 * 2**20, transcendentals=0),
    )(
        *(
            pltpu.with_memory_space_constraint(operand, pltpu.HBM)
            for operand in (matrix, flips.reshape(LANES, LANES), owners, offsets)
        )
    )
    message = pl.pallas_call(
        send_kernel,
        name="transform_and_requests",
        out_shape=message_shape,
        in_specs=[VMEM] * 5,
        out_specs=VMEM,
        scratch_shapes=[pltpu.VMEM((LANES, COLS, LANES), f32)],
        compiler_params=params,
    )(matrix, flips, own, owners_other, offsets_other)
    message = exchange(message, FIRST)
    reply_shape = jax.ShapeDtypeStruct((CHIPS, LANES), f32)
    tables = [pltpu.VMEM((2 * LANES, PICKS), jnp.bfloat16), pltpu.VMEM((CHIPS, PICKS), f32)]
    theirs, left = pl.pallas_call(
        answer_other_kernel,
        name="answer_other",
        out_shape=(reply_shape, jax.ShapeDtypeStruct((HALVES, CHIPS * COLS, 2 * LANES), jnp.bfloat16)),
        in_specs=[VMEM],
        out_specs=(VMEM, VMEM),
        scratch_shapes=tables,
        compiler_params=params,
    )(message)
    theirs = other_core(theirs)
    mine = pl.pallas_call(
        answer_own_kernel,
        name="answer_own",
        out_shape=reply_shape,
        in_specs=[VMEM, VMEM],
        out_specs=VMEM,
        scratch_shapes=tables,
        compiler_params=params,
        cost_estimate=pl.CostEstimate(flops=2**28, bytes_accessed=2**21, transcendentals=0),
    )(message, left)
    reply = exchange(mine + theirs, FIRST_BACK)
    sketch, gram = pl.pallas_call(
        finish_kernel,
        name="finish",
        out_shape=(jax.ShapeDtypeStruct((COLS, PICKS), f32), jax.ShapeDtypeStruct((1, COLS * COLS), f32)),
        in_specs=[VMEM] * 2,
        out_specs=(HBM, HBM),
        scratch_shapes=[
            pltpu.VMEM((COLS, PICKS), f32),
            pltpu.VMEM((1, COLS * COLS), f32),
            pltpu.SemaphoreType.DMA((2,)),
        ],
        compiler_params=params,
    )(reply, slots)
    return sketch, gram.reshape(COLS * COLS, 1)


def solution(mesh):
    flat = Mesh(mesh.devices.reshape(-1), ("all",))
    in_specs = (P(None, "all"), P("all"), P("all", None), P("all"))
    out_specs = (P(None, "all"), P(None, "all"))
    return jax.shard_map(on_device, mesh=flat, in_specs=in_specs, out_specs=out_specs, check_vma=False)
```
